128 devices in a mesh: fsdp: 32 (over z, y, core), tensor: 4 (over x).
Axes of the slice: x: 4, y: 4, z: 4, core: 2. Of those that a mesh axis runs over, the one named last changes fastest.
Arguments:
- gradient: float32 [16, 512, 8192], P(None, 'fsdp', 'tensor'), may hold values from -1500 to 1500
- owner: int32 [16, 16], P(None, 'tensor'), may hold values from 0 to 31, as said below
- slot: int32 [16, 16], P(None, 'tensor'), may hold values from 0 to 3
- left_gram: float32 [512, 512, 512], P(('fsdp', 'tensor')), may hold values from -1 to 1, as said below
- right_gram: float32 [512, 512, 512], P(('fsdp', 'tensor')), may hold values from -1 to 1, as said below
- left_root: bfloat16 [512, 512, 512], P(('fsdp', 'tensor')), may hold values from -1 to 4, as said below
- right_root: bfloat16 [512, 512, 512], P(('fsdp', 'tensor')), may hold values from -1 to 4, as said below
Outputs:
- left_gram_new: float32 [512, 512, 512], P(('fsdp', 'tensor'))
- right_gram_new: float32 [512, 512, 512], P(('fsdp', 'tensor'))
- update: bfloat16 [16, 512, 8192], P(None, 'fsdp', 'tensor')
The draws below stay inside these ranges and needn't reach their ends.
Inputs may be any that keep to these rules, and one draw needn't show every extreme that they name: In every tensor index, no two blocks share an owner and a slot, and some owner holds 4 blocks. `left_gram`: Symmetric. `right_gram`: Symmetric. `left_root`: Symmetric. `right_root`: Symmetric.
All inputs are finite; a program needn't handle non-finite values.
Results may differ from the reference program's by a relative error of at most 0.015.
Values may be sent and summed in bfloat16 or wider, within the bound.
A program may use at most 128 MiB of HBM per device.

```python
import math
import jax
import jax.numpy as jnp
from jax import lax

COLS = 8192
BLOCK = 512
SLOTS = 4
COL_DEV = 2048
NBR = 16
NBC = 16
ALL_SLOTS = 512
N_FSDP = 32
N_TENSOR = 4


def group_positions(key):
    position_count = N_FSDP * SLOTS
    block_count = NBR * (COL_DEV // BLOCK)
    key_full, key_order, key_assign = jax.random.split(key, 3)
    full_owner = jax.random.randint(key_full, (), 0, N_FSDP)
    shuffled = jax.random.permutation(key_order, position_count)
    ranking = jnp.arange(position_count)
    scores = jnp.where(shuffled // SLOTS == full_owner, ranking - position_count, ranking)
    chosen = shuffled[jnp.argsort(scores, stable=True)][:block_count]
    return jax.random.permutation(key_assign, chosen)


def place_blocks(key):
    group_keys = jax.random.split(key, N_TENSOR)
    placed = jax.vmap(group_positions)(group_keys)
    per_group = COL_DEV // BLOCK
    placed = placed.reshape(N_TENSOR, NBR, per_group).transpose(1, 0, 2)
    return placed.reshape(NBR, N_TENSOR * per_group).astype(jnp.int32)


def draw_owner(key, part):
    placed = place_blocks(key)
    return placed // SLOTS


def draw_slot(key, part):
    placed = place_blocks(key)
    return placed % SLOTS


def draw_gradient(key, part):
    key = jax.random.fold_in(key, 5)
    key_base, key_rows, key_cols = jax.random.split(key, 3)
    extent = (NBR, BLOCK, COLS)
    base = jnp.clip(jax.random.normal(key_base, extent, jnp.float32), -4.0, 4.0)
    rising_rows = jnp.exp(0.5 * math.log(3.0) * jnp.arange(BLOCK, dtype=jnp.float32) / BLOCK)
    rising_cols = jnp.exp(0.5 * math.log(3.0) * jnp.arange(COLS, dtype=jnp.float32) / COLS)
    row_scale = jnp.exp(jax.random.uniform(key_rows, (NBR, BLOCK, 1), jnp.float32, 0.0, math.log(10.0)))
    col_scale = jnp.exp(jax.random.uniform(key_cols, (1, 1, COLS), jnp.float32, 0.0, math.log(10.0)))
    row_scale = row_scale * rising_rows[None, :, None]
    col_scale = col_scale * rising_cols[None, None, :]
    return base * row_scale * col_scale


def symmetric_noise(key, scale):
    raw = jnp.clip(jax.random.normal(key, (ALL_SLOTS, BLOCK, BLOCK), jnp.float32), -4.0, 4.0)
    return (raw + jnp.swapaxes(raw, 1, 2)) * (0.5 * scale)


def with_diagonal(key, diagonal, scale):
    identity = jnp.eye(BLOCK, dtype=jnp.float32)
    return symmetric_noise(key, scale) * (1.0 - identity) + identity[None, :, :] * diagonal[:, :, None]


def draw_left_gram(key, part):
    key = jax.random.fold_in(key, 11)
    key_diag, key_noise = jax.random.split(key)
    diagonal = jnp.exp(jax.random.uniform(key_diag, (ALL_SLOTS, BLOCK), jnp.float32, math.log(0.05), math.log(0.5)))
    return with_diagonal(key_noise, diagonal, 0.06 / math.sqrt(BLOCK))


def draw_right_gram(key, part):
    key = jax.random.fold_in(key, 12)
    key_diag, key_noise = jax.random.split(key)
    diagonal = jnp.exp(jax.random.uniform(key_diag, (ALL_SLOTS, BLOCK), jnp.float32, math.log(0.05), math.log(0.5)))
    return with_diagonal(key_noise, diagonal, 0.06 / math.sqrt(BLOCK))


def draw_left_root(key, part):
    key = jax.random.fold_in(key, 13)
    key_diag, key_noise = jax.random.split(key)
    diagonal = jnp.exp(jax.random.uniform(key_diag, (ALL_SLOTS, BLOCK), jnp.float32, 0.0, math.log(4.0)))
    return with_diagonal(key_noise, diagonal, 0.6 / math.sqrt(BLOCK)).astype(jnp.bfloat16)


def draw_right_root(key, part):
    key = jax.random.fold_in(key, 14)
    key_diag, key_noise = jax.random.split(key)
    diagonal = jnp.exp(jax.random.uniform(key_diag, (ALL_SLOTS, BLOCK), jnp.float32, 0.0, math.log(4.0)))
    return with_diagonal(key_noise, diagonal, 0.6 / math.sqrt(BLOCK)).astype(jnp.bfloat16)


def setup_inputs(seed: int = 0) -> dict:
    arg_keys = jax.random.split(jax.random.key(seed), 8)
    gradient = draw_gradient(jax.random.fold_in(arg_keys[7], 71), 0)
    owner = draw_owner(jax.random.fold_in(arg_keys[7], 71), 0)
    slot = draw_slot(jax.random.fold_in(arg_keys[7], 71), 0)
    left_gram = draw_left_gram(jax.random.fold_in(arg_keys[7], 71), 0)
    right_gram = draw_right_gram(jax.random.fold_in(arg_keys[7], 71), 0)
    left_root = draw_left_root(jax.random.fold_in(arg_keys[7], 71), 0)
    right_root = draw_right_root(jax.random.fold_in(arg_keys[7], 71), 0)
    return {"gradient": gradient, "owner": owner, "slot": slot, "left_gram": left_gram, "right_gram": right_gram, "left_root": left_root, "right_root": right_root}


clip_rms = 0.05
eps_norm = 1e-06

def reference(gradient, owner, slot, left_gram, right_gram, left_root, right_root):
    high = lax.Precision.HIGHEST
    mean_square = jnp.mean(gradient * gradient)
    factor = clip_rms / jnp.sqrt(mean_square + eps_norm)
    clipped = gradient * factor
    per_group = COL_DEV // BLOCK
    column_group = (jnp.arange(NBC, dtype=jnp.int32) // per_group)[None, :]
    target = ((owner * N_TENSOR + column_group) * SLOTS + slot).reshape(-1).astype(jnp.int32)
    blocks = clipped.reshape(NBR, BLOCK, NBC, BLOCK).transpose(0, 2, 1, 3).reshape(NBR * NBC, BLOCK, BLOCK)

    def one_block(items):
        matrix, where_to = items
        left_old = lax.dynamic_index_in_dim(left_gram, where_to, 0, keepdims=False)
        right_old = lax.dynamic_index_in_dim(right_gram, where_to, 0, keepdims=False)
        left_inv = lax.dynamic_index_in_dim(left_root, where_to, 0, keepdims=False)
        right_inv = lax.dynamic_index_in_dim(right_root, where_to, 0, keepdims=False)
        left_new = left_old + jnp.dot(matrix, matrix.T, precision=high, preferred_element_type=jnp.float32)
        right_new = right_old + jnp.dot(matrix.T, matrix, precision=high, preferred_element_type=jnp.float32)
        lowered = matrix.astype(jnp.bfloat16)
        left_side = jnp.dot(left_inv, lowered, preferred_element_type=jnp.float32).astype(jnp.bfloat16)
        result = jnp.dot(left_side, right_inv, preferred_element_type=jnp.float32).astype(jnp.bfloat16)
        return (left_new, right_new, result)
    left_new, right_new, results = lax.map(one_block, (blocks, target))
    left_gram_new = left_gram.at[target].set(left_new)
    right_gram_new = right_gram.at[target].set(right_new)
    update = results.reshape(NBR, NBC, BLOCK, BLOCK).transpose(0, 2, 1, 3).reshape(NBR, BLOCK, COLS)
    return (left_gram_new, right_gram_new, update)
```

```python
import functools

import jax
import jax.numpy as jnp
from jax import lax
from jax.experimental import pallas as pl
from jax.experimental.pallas import tpu as pltpu
from jax.sharding import PartitionSpec as P

clip_rms = 0.05
eps_norm = 1e-06
MESH = pl.DeviceIdType.MESH


def peer(me, d):
    z, y, c = me // 8, (me // 2) % 4, me % 2
    z, y, c = (z + d // 8) % 4, (y + (d // 2) % 4) % 4, (c + d % 2) % 2
    return (z * 4 + y) * 2 + c


def exchange_kernel(
    entry_count, owners, tensors, slots, rows, size,
    owner_ref, slot_ref, grad_hbm, lroot_hbm, rroot_hbm,
    arrived, update, gains,
    grad, lroot, rroot, outbox, results, returned, table_v, table_s, side_sums, sums,
    local_sem, table_sem, side_send, side_recv, sum_send, sum_recv, go_send, go_recv, back_send, back_recv,
):
    me = lax.axis_index("fsdp")
    side = lax.axis_index("tensor")
    row_blocks, per_row = owner_ref.shape
    positions = owners * slots

    load_left = pltpu.make_async_copy(lroot_hbm, lroot, local_sem.at[0])
    load_right = pltpu.make_async_copy(rroot_hbm, rroot, local_sem.at[1])
    load_grad = [
        pltpu.make_async_copy(
            grad_hbm.at[:, :, pl.ds(c * size, size)],
            grad.at[pl.ds(c * row_blocks, row_blocks)],
            local_sem.at[2 + c],
        )
        for c in range(per_row)
    ]
    for load in load_grad:
        load.start()
    load_left.start()
    load_right.start()

    barrier = pltpu.get_barrier_semaphore()

    def greet(d, carry):
        pl.semaphore_signal(
            barrier, inc=1, device_id={"fsdp": peer(me, d)}, device_id_type=MESH
        )
        return carry

    lax.fori_loop(1, owners, greet, 0)
    for t in range(1, tensors):
        pl.semaphore_signal(
            barrier, inc=1, device_id={"tensor": (side + t) % tensors}, device_id_type=MESH
        )

    target = owner_ref[...] * slots + slot_ref[...]
    table_v[0:row_blocks, 0:per_row] = target
    lanes = lax.broadcasted_iota(jnp.int32, (row_blocks, positions), 1)
    block_rows = lax.broadcasted_iota(jnp.int32, (row_blocks, positions), 0)
    source = jnp.zeros((row_blocks, positions), jnp.int32)
    filled = jnp.zeros((row_blocks, positions), jnp.float32)
    for c in range(per_row):
        hit = target[:, c : c + 1] == lanes
        source = jnp.where(hit, block_rows + c * row_blocks, source)
        filled = jnp.where(hit, 1.0, filled)
    table_v[row_blocks : row_blocks + 1, :] = jnp.max(source, axis=0, keepdims=True)
    filled = jnp.max(filled, axis=0, keepdims=True)
    load_table = pltpu.make_async_copy(table_v, table_s, table_sem)
    load_table.start()

    for load in load_grad:
        load.wait()

    def square(b, total):
        block = grad[b]
        return total + block * block

    own_sum = lax.fori_loop(0, row_blocks * per_row, square, jnp.zeros((rows, size), jnp.float32))
    own_sum = sum(own_sum[:, k : k + 128] for k in range(0, size, 128))
    side_sums[side] = jnp.sum(own_sum, axis=0, keepdims=True)
    load_table.wait()

    def piece(s, o):
        return grad[table_s[row_blocks, o * slots + s]].astype(jnp.bfloat16)

    my_rows = pl.ds(pl.multiple_of(me * rows, rows), rows)

    def send_slot(s):
        def go(d, carry):
            o = peer(me, d)
            outbox[s, o] = piece(s, o)
            pltpu.make_async_remote_copy(
                src_ref=outbox.at[s, o],
                dst_ref=arrived.at[s, my_rows, :],
                send_sem=go_send.at[s],
                recv_sem=go_recv.at[s],
                device_id={"fsdp": o},
                device_id_type=MESH,
            ).start()
            return carry

        lax.fori_loop(1, owners, go, 0)
        arrived[s, my_rows, :] = piece(s, me)

    def all_of(ref, send_sem, recv_sem):
        some = ref.at[pl.ds(0, owners - 1)]
        return pltpu.make_async_remote_copy(
            src_ref=some, dst_ref=some, send_sem=send_sem, recv_sem=recv_sem,
            device_id={"fsdp": peer(me, 1)}, device_id_type=MESH,
        )

    pl.semaphore_wait(barrier, owners - 1 + tensors - 1)

    for t in range(1, tensors):
        pltpu.make_async_remote_copy(
            src_ref=side_sums.at[side],
            dst_ref=side_sums.at[side],
            send_sem=side_send,
            recv_sem=side_recv,
            device_id={"tensor": (side + t) % tensors},
            device_id_type=MESH,
        ).start()
    send_slot(0)
    some = side_sums.at[pl.ds(0, tensors - 1)]
    side_all = pltpu.make_async_remote_copy(
        src_ref=some, dst_ref=some, send_sem=side_send, recv_sem=side_recv,
        device_id={"tensor": (side + 1) % tensors}, device_id_type=MESH,
    )
    side_all.wait_recv()
    sums[me] = jnp.sum(side_sums[...], axis=0)

    def send_sum(d, carry):
        pltpu.make_async_remote_copy(
            src_ref=sums.at[me],
            dst_ref=sums.at[me],
            send_sem=sum_send,
            recv_sem=sum_recv,
            device_id={"fsdp": peer(me, d)},
            device_id_type=MESH,
        ).start()
        return carry

    lax.fori_loop(1, owners, send_sum, 0)
    for s in range(1, slots):
        send_slot(s)

    sum_all = all_of(sums, sum_send, sum_recv)
    sum_all.wait_recv()
    grand_sum = jnp.sum(jnp.sum(sums[...], axis=0), axis=1, keepdims=True)
    factor = clip_rms / jnp.sqrt(grand_sum / entry_count + eps_norm)
    lane = lax.broadcasted_iota(jnp.int32, (1, positions), 1)
    for s in range(slots):
        mine = jnp.sum(jnp.where(lane == me * slots + s, filled, 0.0), axis=1, keepdims=True)
        gains[s] = jnp.broadcast_to(factor * factor * mine, (1, 128))
    load_left.wait()
    load_right.wait()

    for s in range(slots):
        all_of(outbox.at[s], go_send.at[s], go_recv.at[s]).wait_recv()
        left_side = jnp.dot(
            lroot[s], arrived[s], preferred_element_type=jnp.float32
        ).astype(jnp.bfloat16)
        product = jnp.dot(left_side, rroot[s], preferred_element_type=jnp.float32)
        results[s] = (product * factor).astype(jnp.bfloat16)

        def back(d, carry, s=s):
            f = peer(me, d)
            pltpu.make_async_remote_copy(
                src_ref=results.at[s, pl.ds(pl.multiple_of(f * rows, rows), rows), :],
                dst_ref=returned.at[me * slots + s],
                send_sem=back_send.at[s],
                recv_sem=back_recv.at[s],
                device_id={"fsdp": f},
                device_id_type=MESH,
            ).start()
            return carry

        lax.fori_loop(1, owners, back, 0)
        returned[me * slots + s] = results[s, my_rows, :]

    for s in range(slots):
        all_of(returned, back_send.at[s], back_recv.at[s]).wait_recv()

    def place(r, carry):
        for c in range(per_row):
            update[r, :, c * size : (c + 1) * size] = returned[table_s[r, c]]
        return carry

    lax.fori_loop(0, row_blocks, place, 0)

    side_all.wait_send()
    sum_all.wait_send()
    for s in range(slots):
        all_of(outbox.at[s], go_send.at[s], go_recv.at[s]).wait_send()
        all_of(returned, back_send.at[s], back_recv.at[s]).wait_send()


def grams_kernel(gains, arrived, left, right, left_new, right_new):
    g = arrived[0]
    gain = gains[0][:, 0:1]
    rows_product = lax.dot_general(
        g, g, (((1,), (1,)), ((), ())), preferred_element_type=jnp.float32
    )
    left_new[0] = left[0] + rows_product * gain
    columns_product = lax.dot_general(
        g, g, (((0,), (0,)), ((), ())), preferred_element_type=jnp.float32
    )
    right_new[0] = right[0] + columns_product * gain


def per_device(gradient, owner, slot, left_gram, right_gram, left_root, right_root):
    row_blocks, rows, col_count = gradient.shape
    slots, size, _ = left_gram.shape
    owners, tensors = lax.axis_size("fsdp"), lax.axis_size("tensor")
    positions, per_row = owners * slots, col_count // size
    entry_count = float(row_blocks * rows * col_count * owners * tensors)
    vmem = pl.BlockSpec(memory_space=pltpu.VMEM)
    anywhere = pl.BlockSpec(memory_space=pl.ANY)
    dma = pltpu.SemaphoreType.DMA
    bf16, f32, i32 = jnp.bfloat16, jnp.float32, jnp.int32
    arrived, update, gains = pl.pallas_call(
        functools.partial(exchange_kernel, entry_count, owners, tensors, slots, rows, size),
        out_shape=(
            jax.ShapeDtypeStruct((slots, size, size), bf16),
            jax.ShapeDtypeStruct((row_blocks, rows, col_count), bf16),
            jax.ShapeDtypeStruct((slots, 1, 128), f32),
        ),
        in_specs=[vmem, vmem, anywhere, anywhere, anywhere],
        out_specs=(vmem, vmem, vmem),
        scratch_shapes=[
            pltpu.VMEM((row_blocks * per_row, rows, size), f32),
            pltpu.VMEM((slots, size, size), bf16),
            pltpu.VMEM((slots, size, size), bf16),
            pltpu.VMEM((slots, owners, rows, size), bf16),
            pltpu.VMEM((slots, size, size), bf16),
            pltpu.VMEM((positions, rows, size), bf16),
            pltpu.VMEM((row_blocks + 8, positions), i32),
            pltpu.SMEM((row_blocks + 8, positions), i32),
            pltpu.VMEM((tensors, 1, 128), f32),
            pltpu.VMEM((owners, 1, 128), f32),
            dma((2 + per_row,)), dma, dma, dma, dma, dma,
            dma((slots,)), dma((slots,)), dma((slots,)), dma((slots,)),
        ],
        compiler_params=pltpu.CompilerParams(
            collective_id=0, has_side_effects=True, vmem_limit_bytes=32 * 2**20
        ),
        cost_estimate=pl.CostEstimate(
            flops=4 * slots * size**3, bytes_accessed=12 * 2**20, transcendentals=0
        ),
        name="exchange",
    )(owner, slot, gradient, left_root, right_root)

    def one(*tail):
        return pl.BlockSpec((1, *tail), lambda s: (s, 0, 0))

    block = one(size, size)
    left_new, right_new = pl.pallas_call(
        grams_kernel,
        grid=(slots,),
        out_shape=(jax.ShapeDtypeStruct(left_gram.shape, f32),) * 2,
        in_specs=[one(1, 128), block, block, block],
        out_specs=(block, block),
        compiler_params=pltpu.CompilerParams(vmem_limit_bytes=32 * 2**20),
        cost_estimate=pl.CostEstimate(
            flops=4 * slots * size**3, bytes_accessed=18 * 2**20, transcendentals=0
        ),
        name="grams",
    )(gains, arrived, left_gram, right_gram)
    return (left_new, right_new, update)


def solution(mesh):
    return jax.shard_map(
        per_device,
        mesh=mesh,
        in_specs=(
            P(None, "fsdp", "tensor"),
            P(None, "tensor"),
            P(None, "tensor"),
            P(("fsdp", "tensor"), None, None),
            P(("fsdp", "tensor"), None, None),
            P(("fsdp", "tensor"), None, None),
            P(("fsdp", "tensor"), None, None),
        ),
        out_specs=(
            P(("fsdp", "tensor"), None, None),
            P(("fsdp", "tensor"), None, None),
            P(None, "fsdp", "tensor"),
        ),
        check_vma=False,
    )
```

```python
import functools

import jax
import jax.numpy as jnp
from jax import lax
from jax.experimental import pallas as pl
from jax.experimental.pallas import tpu as pltpu
from jax.sharding import PartitionSpec as P

clip_rms = 0.05
eps_norm = 1e-06
MESH = pl.DeviceIdType.MESH


def peer(me, d):
    z, y, c = me // 8, (me // 2) % 4, me % 2
    z, y, c = (z + d // 8) % 4, (y + (d // 2) % 4) % 4, (c + d % 2) % 2
    return (z * 4 + y) * 2 + c


def exchange_kernel(
    entry_count, owners, tensors, slots, rows, size,
    owner_hbm, slot_hbm, grad_hbm, lroot_hbm, rroot_hbm, lgram_hbm, rgram_hbm,
    left_new, right_new, returned,
    owner_ref, slot_ref, grad, lroot, rroot, outbox, arrived, results, table_v, table_s, side_sums, sums,
    local_sem, table_sem, side_send, side_recv, sum_send, sum_recv, go_send, go_recv, back_send, back_recv,
):
    me = lax.axis_index("fsdp")
    side = lax.axis_index("tensor")
    per_row, row_blocks = owner_ref.shape
    positions = owners * slots

    load_left = pltpu.make_async_copy(lroot_hbm, lroot, local_sem.at[0])
    load_right = pltpu.make_async_copy(rroot_hbm, rroot, local_sem.at[1])
    load_lgram = pltpu.make_async_copy(lgram_hbm, left_new, local_sem.at[2])
    load_rgram = pltpu.make_async_copy(rgram_hbm, right_new, local_sem.at[3])
    load_grad = [
        pltpu.make_async_copy(
            grad_hbm.at[:, :, pl.ds(c * size, size)],
            grad.at[pl.ds(c * row_blocks, row_blocks)],
            local_sem.at[4 + c],
        )
        for c in range(per_row)
    ]
    load_tables = [
        pltpu.make_async_copy(owner_hbm, owner_ref, local_sem.at[4 + per_row]),
        pltpu.make_async_copy(slot_hbm, slot_ref, local_sem.at[5 + per_row]),
    ]
    for load in load_tables + load_grad:
        load.start()

    barrier = pltpu.get_barrier_semaphore()

    def greet(d, carry):
        pl.semaphore_signal(
            barrier, inc=1, device_id={"fsdp": peer(me, d)}, device_id_type=MESH
        )
        return carry

    lax.fori_loop(1, owners, greet, 0)
    for t in range(1, tensors):
        pl.semaphore_signal(
            barrier, inc=1, device_id={"tensor": (side + t) % tensors}, device_id_type=MESH
        )

    for load in load_tables:
        load.wait()
    target = owner_ref[...] * slots + slot_ref[...]
    lanes = lax.broadcasted_iota(jnp.int32, (row_blocks, positions), 1)
    block_rows = lax.broadcasted_iota(jnp.int32, (row_blocks, positions), 0)
    source = jnp.zeros((row_blocks, positions), jnp.int32)
    filled = jnp.zeros((row_blocks, positions), jnp.float32)
    target = target.T
    for c in range(per_row):
        hit = target[:, c : c + 1] == lanes
        source = jnp.where(hit, block_rows + c * row_blocks, source)
        filled = jnp.where(hit, 1.0, filled)
    table_v[...] = jnp.max(source, axis=0, keepdims=True)
    filled = jnp.max(filled, axis=0, keepdims=True)
    load_table = pltpu.make_async_copy(table_v, table_s, table_sem)
    load_table.start()

    for load in load_grad:
        load.wait()

    def square(b, total):
        block = grad[b]
        return total + block * block

    own_sum = lax.fori_loop(0, row_blocks * per_row, square, jnp.zeros((rows, size), jnp.float32))
    own_sum = sum(own_sum[:, k : k + 128] for k in range(0, size, 128))
    side_sums[side] = jnp.sum(own_sum, axis=0, keepdims=True)
    load_table.wait()
    for load in (load_left, load_right, load_lgram, load_rgram):
        load.start()

    def piece(s, o):
        return grad[table_s[0, o * slots + s]].astype(jnp.bfloat16)

    my_rows = pl.ds(pl.multiple_of(me * rows, rows), rows)

    def send_slot(s):
        def go(d, carry):
            o = peer(me, d)
            outbox[s, o] = piece(s, o)
            pltpu.make_async_remote_copy(
                src_ref=outbox.at[s, o],
                dst_ref=arrived.at[s, my_rows, :],
                send_sem=go_send.at[s],
                recv_sem=go_recv.at[s],
                device_id={"fsdp": o},
                device_id_type=MESH,
            ).start()
            return carry

        lax.fori_loop(1, owners, go, 0)
        arrived[s, my_rows, :] = piece(s, me)

    def all_of(ref, send_sem, recv_sem):
        some = ref.at[pl.ds(0, owners - 1)]
        return pltpu.make_async_remote_copy(
            src_ref=some, dst_ref=some, send_sem=send_sem, recv_sem=recv_sem,
            device_id={"fsdp": peer(me, 1)}, device_id_type=MESH,
        )

    pl.semaphore_wait(barrier, owners - 1 + tensors - 1)

    for t in range(1, tensors):
        pltpu.make_async_remote_copy(
            src_ref=side_sums.at[side],
            dst_ref=side_sums.at[side],
            send_sem=side_send,
            recv_sem=side_recv,
            device_id={"tensor": (side + t) % tensors},
            device_id_type=MESH,
        ).start()
    send_slot(0)
    some = side_sums.at[pl.ds(0, tensors - 1)]
    side_all = pltpu.make_async_remote_copy(
        src_ref=some, dst_ref=some, send_sem=side_send, recv_sem=side_recv,
        device_id={"tensor": (side + 1) % tensors}, device_id_type=MESH,
    )
    side_all.wait_recv()
    sums[me] = jnp.sum(side_sums[...], axis=0)

    def send_sum(d, carry):
        pltpu.make_async_remote_copy(
            src_ref=sums.at[me],
            dst_ref=sums.at[me],
            send_sem=sum_send,
            recv_sem=sum_recv,
            device_id={"fsdp": peer(me, d)},
            device_id_type=MESH,
        ).start()
        return carry

    lax.fori_loop(1, owners, send_sum, 0)
    for s in range(1, slots):
        send_slot(s)

    sum_all = all_of(sums, sum_send, sum_recv)
    sum_all.wait_recv()
    grand_sum = jnp.sum(jnp.sum(sums[...], axis=0), axis=1, keepdims=True)
    factor = clip_rms / jnp.sqrt(grand_sum / entry_count + eps_norm)
    lane = lax.broadcasted_iota(jnp.int32, (1, positions), 1)
    gain = []
    for s in range(slots):
        mine = jnp.sum(jnp.where(lane == me * slots + s, filled, 0.0), axis=1, keepdims=True)
        gain.append(factor * factor * mine)
    load_left.wait()
    load_right.wait()

    for s in range(slots):
        all_of(outbox.at[s], go_send.at[s], go_recv.at[s]).wait_recv()
        left_side = jnp.dot(
            lroot[s], arrived[s], preferred_element_type=jnp.float32
        ).astype(jnp.bfloat16)
        product = jnp.dot(left_side, rroot[s], preferred_element_type=jnp.float32)
        results[s] = (product * factor).astype(jnp.bfloat16)

        def back(d, carry, s=s):
            f = peer(me, d)
            pltpu.make_async_remote_copy(
                src_ref=results.at[s, pl.ds(pl.multiple_of(f * rows, rows), rows), :],
                dst_ref=returned.at[me * slots + s],
                send_sem=back_send.at[s],
                recv_sem=back_recv.at[s],
                device_id={"fsdp": f},
                device_id_type=MESH,
            ).start()
            return carry

        lax.fori_loop(1, owners, back, 0)
        returned[me * slots + s] = results[s, my_rows, :]

    load_lgram.wait()
    load_rgram.wait()
    for s in range(slots):
        g = arrived[s]
        left_new[s] += gain[s] * lax.dot_general(
            g, g, (((1,), (1,)), ((), ())), preferred_element_type=jnp.float32
        )
        right_new[s] += gain[s] * lax.dot_general(
            g, g, (((0,), (0,)), ((), ())), preferred_element_type=jnp.float32
        )

    for s in range(slots):
        all_of(returned, back_send.at[s], back_recv.at[s]).wait_recv()

    side_all.wait_send()
    sum_all.wait_send()
    for s in range(slots):
        all_of(outbox.at[s], go_send.at[s], go_recv.at[s]).wait_send()
        all_of(returned, back_send.at[s], back_recv.at[s]).wait_send()


def finish_kernel(
    slots, owner_hbm, slot_hbm, left, right, returned, left_new, right_new, update,
    owner, slot, placed, sems, table_sems,
):
    load_owner = pltpu.make_async_copy(owner_hbm, owner, table_sems.at[0])
    load_slot = pltpu.make_async_copy(slot_hbm, slot, table_sems.at[1])
    load_owner.start()
    load_slot.start()
    per_row, row_blocks = owner.shape
    size = left.shape[-1]
    copies = []
    for s in range(slots):
        for ref, new in ((left, left_new), (right, right_new)):
            copies.append(pltpu.make_async_copy(ref.at[s], new.at[s], sems.at[len(copies)]))
            copies[-1].start()

    def place(r, carry):
        for c in range(per_row):
            placed[r, :, c * size : (c + 1) * size] = returned[owner[c, r] * slots + slot[c, r]]
        return carry

    load_owner.wait()
    load_slot.wait()
    quarter = row_blocks // 4
    for k in range(0, row_blocks, quarter):
        lax.fori_loop(k, k + quarter, place, 0)
        part = pl.ds(k, quarter)
        copies.append(pltpu.make_async_copy(placed.at[part], update.at[part], sems.at[len(copies)]))
        copies[-1].start()
    for copy in copies:
        copy.wait()


def per_device(gradient, owner, slot, left_gram, right_gram, left_root, right_root):
    row_blocks, rows, col_count = gradient.shape
    slots, size, _ = left_gram.shape
    owners, tensors = lax.axis_size("fsdp"), lax.axis_size("tensor")
    positions, per_row = owners * slots, col_count // size
    entry_count = float(row_blocks * rows * col_count * owners * tensors)
    vmem = pl.BlockSpec(memory_space=pltpu.VMEM)
    dma = pltpu.SemaphoreType.DMA
    bf16, f32, i32 = jnp.bfloat16, jnp.float32, jnp.int32
    hbm = pl.BlockSpec(memory_space=pltpu.HBM)
    owner, slot = owner.T, slot.T
    big = [
        pltpu.with_memory_space_constraint(x, pltpu.HBM)
        for x in (owner, slot, gradient, left_root, right_root, left_gram, right_gram)
    ]
    left, right, returned = pl.pallas_call(
        functools.partial(exchange_kernel, entry_count, owners, tensors, slots, rows, size),
        out_shape=(
            pltpu.VMEM((slots, size, size), f32),
            pltpu.VMEM((slots, size, size), f32),
            pltpu.VMEM((positions, rows, size), bf16),
        ),
        in_specs=[hbm] * 7,
        out_specs=(vmem, vmem, vmem),
        scratch_shapes=[
            pltpu.VMEM((per_row, row_blocks), i32),
            pltpu.VMEM((per_row, row_blocks), i32),
            pltpu.VMEM((row_blocks * per_row, rows, size), f32),
            pltpu.VMEM((slots, size, size), bf16),
            pltpu.VMEM((slots, size, size), bf16),
            pltpu.VMEM((slots, owners, rows, size), bf16),
            pltpu.VMEM((slots, size, size), bf16),
            pltpu.VMEM((slots, size, size), bf16),
            pltpu.VMEM((1, positions), i32),
            pltpu.SMEM((1, positions), i32),
            pltpu.VMEM((tensors, 1, 128), f32),
            pltpu.VMEM((owners, 1, 128), f32),
            dma((6 + per_row,)), dma, dma, dma, dma, dma,
            dma((slots,)), dma((slots,)), dma((slots,)), dma((slots,)),
        ],
        compiler_params=pltpu.CompilerParams(
            collective_id=0, has_side_effects=True, vmem_limit_bytes=32 * 2**20
        ),
        cost_estimate=pl.CostEstimate(
            flops=8 * slots * size**3, bytes_accessed=24 * 2**20, transcendentals=0
        ),
        name="exchange",
    )(*big)
    return pl.pallas_call(
        functools.partial(finish_kernel, slots),
        out_shape=(
            jax.ShapeDtypeStruct(left_gram.shape, f32),
            jax.ShapeDtypeStruct(right_gram.shape, f32),
            jax.ShapeDtypeStruct(gradient.shape, bf16),
        ),
        in_specs=[hbm, hbm, vmem, vmem, vmem],
        out_specs=(hbm, hbm, hbm),
        scratch_shapes=[
            pltpu.SMEM(owner.shape, i32),
            pltpu.SMEM(owner.shape, i32),
            pltpu.VMEM(gradient.shape, bf16),
            dma((2 * slots + 4,)),
            dma((2,)),
        ],
        compiler_params=pltpu.CompilerParams(vmem_limit_bytes=24 * 2**20),
        cost_estimate=pl.CostEstimate(flops=0, bytes_accessed=9 * 2**20, transcendentals=0),
        name="finish",
    )(*big[:2], left, right, returned)


def solution(mesh):
    return jax.shard_map(
        per_device,
        mesh=mesh,
        in_specs=(
            P(None, "fsdp", "tensor"),
            P(None, "tensor"),
            P(None, "tensor"),
            P(("fsdp", "tensor"), None, None),
            P(("fsdp", "tensor"), None, None),
            P(("fsdp", "tensor"), None, None),
            P(("fsdp", "tensor"), None, None),
        ),
        out_specs=(
            P(("fsdp", "tensor"), None, None),
            P(("fsdp", "tensor"), None, None),
            P(None, "fsdp", "tensor"),
        ),
        check_vma=False,
    )
```

```python
import functools

import jax
import jax.numpy as jnp
from jax import lax
from jax.experimental import pallas as pl
from jax.experimental.pallas import tpu as pltpu
from jax.sharding import PartitionSpec as P

clip_rms = 0.05
eps_norm = 1e-06
MESH = pl.DeviceIdType.MESH
ORDER = ((0, 0), (1, 1), (2, 2), (3, 9))


def peer(me, d):
    z, y, c = me // 8, (me // 2) % 4, me % 2
    z, y, c = (z + d // 8) % 4, (y + (d // 2) % 4) % 4, (c + d % 2) % 2
    return (z * 4 + y) * 2 + c


def exchange_kernel(
    entry_count, owners, tensors, slots, rows, size,
    owner_hbm, slot_hbm, grad_hbm, lroot_hbm, rroot_hbm, lgram_hbm, rgram_hbm,
    left_new, right_new, returned,
    owner_ref, slot_ref, grad, lroot, rroot, outbox, arrived, results, table_v, table_s, side_sums, sums,
    local_sem, table_sem, side_send, side_recv, sum_send, sum_recv, go_send, go_recv, back_send, back_recv,
):
    me = lax.axis_index("fsdp")
    side = lax.axis_index("tensor")
    per_row, row_blocks = owner_ref.shape
    positions = owners * slots

    load_left = pltpu.make_async_copy(lroot_hbm, lroot, local_sem.at[0])
    load_right = pltpu.make_async_copy(rroot_hbm, rroot, local_sem.at[1])
    load_lgram = pltpu.make_async_copy(lgram_hbm, left_new, local_sem.at[2])
    load_rgram = pltpu.make_async_copy(rgram_hbm, right_new, local_sem.at[3])
    load_grad = [
        pltpu.make_async_copy(
            grad_hbm.at[:, :, pl.ds(c * size, size)],
            grad.at[pl.ds(c * row_blocks, row_blocks)],
            local_sem.at[4 + c],
        )
        for c in range(per_row)
    ]
    load_tables = [
        pltpu.make_async_copy(owner_hbm, owner_ref, local_sem.at[4 + per_row]),
        pltpu.make_async_copy(slot_hbm, slot_ref, local_sem.at[5 + per_row]),
    ]
    for load in load_tables + load_grad:
        load.start()

    barrier = pltpu.get_barrier_semaphore()

    for i in range(1, owners):
        pl.semaphore_signal(
            barrier, inc=1, device_id={"fsdp": (me + i) % owners}, device_id_type=MESH
        )
    for t in range(1, tensors):
        pl.semaphore_signal(
            barrier, inc=1, device_id={"tensor": (side + t) % tensors}, device_id_type=MESH
        )

    for load in load_tables:
        load.wait()
    target = owner_ref[...] * slots + slot_ref[...]
    lanes = lax.broadcasted_iota(jnp.int32, (row_blocks, positions), 1)
    block_rows = lax.broadcasted_iota(jnp.int32, (row_blocks, positions), 0)
    source = jnp.zeros((row_blocks, positions), jnp.int32)
    filled = jnp.zeros((row_blocks, positions), jnp.float32)
    target = target.T
    for c in range(per_row):
        hit = target[:, c : c + 1] == lanes
        source = jnp.where(hit, block_rows + c * row_blocks, source)
        filled = jnp.where(hit, 1.0, filled)
    table_v[...] = jnp.max(source, axis=0, keepdims=True)
    filled = jnp.max(filled, axis=0, keepdims=True)
    load_table = pltpu.make_async_copy(table_v, table_s, table_sem)
    load_table.start()

    for load in load_grad:
        load.wait()
    load_table.wait()
    for load in (load_left, load_right, load_lgram, load_rgram):
        load.start()

    def piece(s, o):
        return grad[table_s[0, o * slots + s]].astype(jnp.bfloat16)

    my_rows = pl.ds(pl.multiple_of(me * rows, rows), rows)

    def send_slot(s):
        def go(d, carry):
            o = peer(me, d)
            outbox[s, o] = piece(s, o)
            pltpu.make_async_remote_copy(
                src_ref=outbox.at[s, o],
                dst_ref=arrived.at[s, my_rows, :],
                send_sem=go_send.at[s],
                recv_sem=go_recv.at[s],
                device_id={"fsdp": o},
                device_id_type=MESH,
            ).start()
            return carry

        lax.fori_loop(1, owners, go, 0)
        arrived[s, my_rows, :] = piece(s, me)

    def all_of(ref, send_sem, recv_sem):
        some = ref.at[pl.ds(0, owners - 1)]
        return pltpu.make_async_remote_copy(
            src_ref=some, dst_ref=some, send_sem=send_sem, recv_sem=recv_sem,
            device_id={"fsdp": peer(me, 1)}, device_id_type=MESH,
        )

    pl.semaphore_wait(barrier, owners - 1 + tensors - 1)

    send_slot(0)

    def square(b, total):
        block = grad[b]
        return total + block * block

    own_sum = lax.fori_loop(0, row_blocks * per_row, square, jnp.zeros((rows, size), jnp.float32))
    own_sum = sum(own_sum[:, k : k + 128] for k in range(0, size, 128))
    side_sums[side] = jnp.sum(own_sum, axis=0, keepdims=True)
    for t in range(1, tensors):
        pltpu.make_async_remote_copy(
            src_ref=side_sums.at[side],
            dst_ref=side_sums.at[side],
            send_sem=side_send,
            recv_sem=side_recv,
            device_id={"tensor": (side + t) % tensors},
            device_id_type=MESH,
        ).start()
    send_slot(1)
    some = side_sums.at[pl.ds(0, tensors - 1)]
    side_all = pltpu.make_async_remote_copy(
        src_ref=some, dst_ref=some, send_sem=side_send, recv_sem=side_recv,
        device_id={"tensor": (side + 1) % tensors}, device_id_type=MESH,
    )
    side_all.wait_recv()
    sums[me] = jnp.sum(side_sums[...], axis=0)

    def send_sum(d, carry):
        pltpu.make_async_remote_copy(
            src_ref=sums.at[me],
            dst_ref=sums.at[me],
            send_sem=sum_send,
            recv_sem=sum_recv,
            device_id={"fsdp": peer(me, d)},
            device_id_type=MESH,
        ).start()
        return carry

    lax.fori_loop(1, owners, send_sum, 0)
    for s in range(2, slots):
        send_slot(s)

    sum_all = all_of(sums, sum_send, sum_recv)
    sum_all.wait_recv()
    grand_sum = jnp.sum(jnp.sum(sums[...], axis=0), axis=1, keepdims=True)
    factor = clip_rms / jnp.sqrt(grand_sum / entry_count + eps_norm)
    lane = lax.broadcasted_iota(jnp.int32, (1, positions), 1)
    gain = []
    for s in range(slots):
        mine = jnp.sum(jnp.where(lane == me * slots + s, filled, 0.0), axis=1, keepdims=True)
        gain.append(factor * factor * mine)
    load_left.wait()
    load_right.wait()

    def send_back(s, low, high):
        def back(d, carry):
            f = peer(me, d)
            z, y = f // 8, (f // 2) % 4
            far = jnp.minimum(z, 4 - z) + jnp.minimum(y, 4 - y)

            @pl.when((far >= low) & (far <= high))
            def _():
                pltpu.make_async_remote_copy(
                    src_ref=results.at[s, pl.ds(pl.multiple_of(f * rows, rows), rows), :],
                    dst_ref=returned.at[me * slots + s],
                    send_sem=back_send.at[s],
                    recv_sem=back_recv.at[s],
                    device_id={"fsdp": f},
                    device_id_type=MESH,
                ).start()

            return carry

        lax.fori_loop(1, owners, back, 0)

    for s in range(slots):
        all_of(outbox.at[s], go_send.at[s], go_recv.at[s]).wait_recv()
        left_side = jnp.dot(
            lroot[s], arrived[s], preferred_element_type=jnp.float32
        ).astype(jnp.bfloat16)
        product = jnp.dot(left_side, rroot[s], preferred_element_type=jnp.float32)
        results[s] = (product * factor).astype(jnp.bfloat16)

        for low, high in ORDER if s == slots - 1 else ((0, 9),):
            send_back(s, low, high)
        returned[me * slots + s] = results[s, my_rows, :]

    load_lgram.wait()
    load_rgram.wait()
    for s in range(slots):
        g = arrived[s]
        left_new[s] += gain[s] * lax.dot_general(
            g, g, (((1,), (1,)), ((), ())), preferred_element_type=jnp.float32
        )
        right_new[s] += gain[s] * lax.dot_general(
            g, g, (((0,), (0,)), ((), ())), preferred_element_type=jnp.float32
        )

    for s in range(slots):
        all_of(returned, back_send.at[s], back_recv.at[s]).wait_recv()

    side_all.wait_send()
    sum_all.wait_send()
    for s in range(slots):
        all_of(outbox.at[s], go_send.at[s], go_recv.at[s]).wait_send()
        all_of(returned, back_send.at[s], back_recv.at[s]).wait_send()


def finish_kernel(
    slots, owner_hbm, slot_hbm, left, right, returned, left_new, right_new, update,
    owner, slot, placed, sems, table_sems,
):
    load_owner = pltpu.make_async_copy(owner_hbm, owner, table_sems.at[0])
    load_slot = pltpu.make_async_copy(slot_hbm, slot, table_sems.at[1])
    load_owner.start()
    load_slot.start()
    per_row, row_blocks = owner.shape
    size = left.shape[-1]
    copies = []
    for s in range(slots):
        for ref, new in ((left, left_new), (right, right_new)):
            copies.append(pltpu.make_async_copy(ref.at[s], new.at[s], sems.at[len(copies)]))
            copies[-1].start()

    def place(r, carry):
        for c in range(per_row):
            placed[r, :, c * size : (c + 1) * size] = returned[owner[c, r] * slots + slot[c, r]]
        return carry

    load_owner.wait()
    load_slot.wait()
    quarter = row_blocks // 4
    for k in range(0, row_blocks, quarter):
        lax.fori_loop(k, k + quarter, place, 0)
        part = pl.ds(k, quarter)
        copies.append(pltpu.make_async_copy(placed.at[part], update.at[part], sems.at[len(copies)]))
        copies[-1].start()
    for copy in copies:
        copy.wait()


def per_device(gradient, owner, slot, left_gram, right_gram, left_root, right_root):
    row_blocks, rows, col_count = gradient.shape
    slots, size, _ = left_gram.shape
    owners, tensors = lax.axis_size("fsdp"), lax.axis_size("tensor")
    positions, per_row = owners * slots, col_count // size
    entry_count = float(row_blocks * rows * col_count * owners * tensors)
    vmem = pl.BlockSpec(memory_space=pltpu.VMEM)
    dma = pltpu.SemaphoreType.DMA
    bf16, f32, i32 = jnp.bfloat16, jnp.float32, jnp.int32
    hbm = pl.BlockSpec(memory_space=pltpu.HBM)
    owner, slot = owner.T, slot.T
    big = [
        pltpu.with_memory_space_constraint(x, pltpu.HBM)
        for x in (owner, slot, gradient, left_root, right_root, left_gram, right_gram)
    ]
    left, right, returned = pl.pallas_call(
        functools.partial(exchange_kernel, entry_count, owners, tensors, slots, rows, size),
        out_shape=(
            pltpu.VMEM((slots, size, size), f32),
            pltpu.VMEM((slots, size, size), f32),
            pltpu.VMEM((positions, rows, size), bf16),
        ),
        in_specs=[hbm] * 7,
        out_specs=(vmem, vmem, vmem),
        scratch_shapes=[
            pltpu.VMEM((per_row, row_blocks), i32),
            pltpu.VMEM((per_row, row_blocks), i32),
            pltpu.VMEM((row_blocks * per_row, rows, size), f32),
            pltpu.VMEM((slots, size, size), bf16),
            pltpu.VMEM((slots, size, size), bf16),
            pltpu.VMEM((slots, owners, rows, size), bf16),
            pltpu.VMEM((slots, size, size), bf16),
            pltpu.VMEM((slots, size, size), bf16),
            pltpu.VMEM((1, positions), i32),
            pltpu.SMEM((1, positions), i32),
            pltpu.VMEM((tensors, 1, 128), f32),
            pltpu.VMEM((owners, 1, 128), f32),
            dma((6 + per_row,)), dma, dma, dma, dma, dma,
            dma((slots,)), dma((slots,)), dma((slots,)), dma((slots,)),
        ],
        compiler_params=pltpu.CompilerParams(
            collective_id=0, has_side_effects=True, vmem_limit_bytes=32 * 2**20
        ),
        cost_estimate=pl.CostEstimate(
            flops=8 * slots * size**3, bytes_accessed=24 * 2**20, transcendentals=0
        ),
        name="exchange",
    )(*big)
    return pl.pallas_call(
        functools.partial(finish_kernel, slots),
        out_shape=(
            jax.ShapeDtypeStruct(left_gram.shape, f32),
            jax.ShapeDtypeStruct(right_gram.shape, f32),
            jax.ShapeDtypeStruct(gradient.shape, bf16),
        ),
        in_specs=[hbm, hbm, vmem, vmem, vmem],
        out_specs=(hbm, hbm, hbm),
        scratch_shapes=[
            pltpu.SMEM(owner.shape, i32),
            pltpu.SMEM(owner.shape, i32),
            pltpu.VMEM(gradient.shape, bf16),
            dma((2 * slots + 4,)),
            dma((2,)),
        ],
        compiler_params=pltpu.CompilerParams(vmem_limit_bytes=24 * 2**20),
        cost_estimate=pl.CostEstimate(flops=0, bytes_accessed=9 * 2**20, transcendentals=0),
        name="finish",
    )(*big[:2], left, right, returned)


def solution(mesh):
    return jax.shard_map(
        per_device,
        mesh=mesh,
        in_specs=(
            P(None, "fsdp", "tensor"),
            P(None, "tensor"),
            P(None, "tensor"),
            P(("fsdp", "tensor"), None, None),
            P(("fsdp", "tensor"), None, None),
            P(("fsdp", "tensor"), None, None),
            P(("fsdp", "tensor"), None, None),
        ),
        out_specs=(
            P(("fsdp", "tensor"), None, None),
            P(("fsdp", "tensor"), None, None),
            P(None, "fsdp", "tensor"),
        ),
        check_vma=False,
    )
```

```python
import functools

import jax
import jax.numpy as jnp
from jax import lax
from jax.experimental import pallas as pl
from jax.experimental.pallas import tpu as pltpu
from jax.sharding import PartitionSpec as P

clip_rms = 0.05
eps_norm = 1e-06
MESH = pl.DeviceIdType.MESH


def exchange_kernel(
    entry_count, owners, tensors, slots, rows, size,
    owner_hbm, slot_hbm, grad_hbm, lroot_hbm, rroot_hbm, lgram_hbm, rgram_hbm,
    left_new, right_new, returned, scale,
    owner_ref, slot_ref, grad, lroot, rroot, own, give, take, arrived, results, back_take,
    table_v, table_s, side_sums, sums, halves, total,
    local_sem, table_sem, side_send, side_recv, sum_send, sum_recv, half_send, half_recv, total_send, total_recv,
    give_send, give_recv, go_send, go_recv, back_give_send, back_give_recv, back_send, back_recv,
):
    me = lax.axis_index("fsdp")
    side = lax.axis_index("tensor")
    per_row, row_blocks = owner_ref.shape
    positions = owners * slots
    chips = owners // 2
    chip, core = me // 2, me % 2
    mate = chip * 2 + 1 - core

    barrier = pltpu.get_barrier_semaphore()
    for i in range(1, chips):
        pl.semaphore_signal(
            barrier, inc=1, device_id={"fsdp": (chip + i) % chips * 2 + core}, device_id_type=MESH
        )
    pl.semaphore_signal(barrier, inc=1, device_id={"fsdp": mate}, device_id_type=MESH)

    speaker = 5

    @pl.when(chip == speaker)
    def _():
        for t in range(1, tensors):
            pl.semaphore_signal(
                barrier, inc=1, device_id={"tensor": (side + t) % tensors}, device_id_type=MESH
            )

    load_left = pltpu.make_async_copy(lroot_hbm, lroot, local_sem.at[0])
    load_right = pltpu.make_async_copy(rroot_hbm, rroot, local_sem.at[1])
    load_lgram = pltpu.make_async_copy(lgram_hbm, left_new, local_sem.at[2])
    load_rgram = pltpu.make_async_copy(rgram_hbm, right_new, local_sem.at[3])
    load_grad = [
        pltpu.make_async_copy(
            grad_hbm.at[:, :, pl.ds(c * size, size)],
            grad.at[pl.ds(c * row_blocks, row_blocks)],
            local_sem.at[4 + c],
        )
        for c in range(per_row)
    ]
    load_tables = [
        pltpu.make_async_copy(owner_hbm, owner_ref, local_sem.at[4 + per_row]),
        pltpu.make_async_copy(slot_hbm, slot_ref, local_sem.at[5 + per_row]),
    ]
    for load in load_tables + load_grad:
        load.start()

    for load in load_tables:
        load.wait()
    target = owner_ref[...] * slots + slot_ref[...]
    lanes = lax.broadcasted_iota(jnp.int32, (row_blocks, positions), 1)
    block_rows = lax.broadcasted_iota(jnp.int32, (row_blocks, positions), 0)
    source = jnp.zeros((row_blocks, positions), jnp.int32)
    filled = jnp.zeros((row_blocks, positions), jnp.float32)
    target = target.T
    for c in range(per_row):
        hit = target[:, c : c + 1] == lanes
        source = jnp.where(hit, block_rows + c * row_blocks, source)
        filled = jnp.where(hit, 1.0, filled)
    table_v[...] = jnp.max(source, axis=0, keepdims=True)
    filled = jnp.max(filled, axis=0, keepdims=True)
    load_table = pltpu.make_async_copy(table_v, table_s, table_sem)
    load_table.start()

    for load in load_grad:
        load.wait()
    load_table.wait()
    for load in (load_left, load_right, load_lgram, load_rgram):
        load.start()

    def piece(s, o):
        return grad[table_s[0, o * slots + s]].astype(jnp.bfloat16)

    def rows_of(f):
        return pl.ds(pl.multiple_of(f * rows, rows), rows)

    def chip_at(d):
        return (chip // 4 + d // 4) % 4 * 4 + (chip % 4 + d % 4) % 4

    def send(src, dst, send_sem, recv_sem, **to):
        copy = pltpu.make_async_remote_copy(
            src_ref=src, dst_ref=dst, send_sem=send_sem, recv_sem=recv_sem,
            device_id=to, device_id_type=MESH,
        )
        copy.start()
        return copy

    def all_of(some, send_sem, recv_sem):
        return pltpu.make_async_remote_copy(
            src_ref=some, dst_ref=some, send_sem=send_sem, recv_sem=recv_sem,
            device_id={"fsdp": mate}, device_id_type=MESH,
        )

    def fill_give(s):
        def fill(k, carry):
            give[s, k] = piece(s, k * 2 + 1 - core)
            return carry

        lax.fori_loop(0, chips, fill, 0)

    def send_give(s):
        send(give.at[s], take.at[s], give_send.at[s], give_recv.at[s], fsdp=mate)

    def send_own(s):
        def go(d, carry):
            k = chip_at(d)
            o = k * 2 + core
            own[s, k] = piece(s, o)
            send(own.at[s, k], arrived.at[s, rows_of(me), :], go_send.at[s], go_recv.at[s], fsdp=o)
            return carry

        lax.fori_loop(1, chips, go, 0)
        arrived[s, rows_of(me), :] = piece(s, me)

    def send_take(s):
        all_of(take.at[s], give_send.at[s], give_recv.at[s]).wait_recv()

        def go(d, carry):
            k = chip_at(d)
            send(
                take.at[s, k], arrived.at[s, rows_of(mate), :], go_send.at[s], go_recv.at[s],
                fsdp=k * 2 + core,
            )
            return carry

        lax.fori_loop(1, chips, go, 0)
        arrived[s, rows_of(mate), :] = take[s, chip]

    fill_give(0)
    pl.semaphore_wait(barrier, chips + jnp.where(chip == speaker, tensors - 1, 0))

    send_give(0)
    send_own(0)
    fill_give(1)
    send_give(1)

    def square(b, total):
        block = grad[b]
        return total + block * block

    own_sum = lax.fori_loop(0, row_blocks * per_row, square, jnp.zeros((rows, size), jnp.float32))
    own_sum = sum(own_sum[:, k : k + 128] for k in range(0, size, 128))
    sums[chip] = jnp.sum(own_sum, axis=0, keepdims=True)

    def send_sum(d, carry):
        send(sums.at[chip], sums.at[chip], sum_send, sum_recv, fsdp=chip_at(d) * 2 + core)
        return carry

    lax.fori_loop(1, chips, send_sum, 0)
    send_take(0)
    send_own(1)
    fill_give(2)
    send_give(2)
    send_take(1)
    sum_all = all_of(sums.at[pl.ds(0, chips - 1)], sum_send, sum_recv)
    sum_all.wait_recv()
    halves[core] = jnp.sum(sums[...], axis=0)
    half = send(halves.at[core], halves.at[core], half_send, half_recv, fsdp=mate)
    send_own(2)
    fill_give(3)
    send_give(3)
    half.wait_recv()
    side_sums[side] = halves[0] + halves[1]
    side_all = all_of(side_sums.at[pl.ds(0, tensors - 1)], side_send, side_recv)

    @pl.when(chip == speaker)
    def _():
        for t in range(1, tensors):
            send(
                side_sums.at[side], side_sums.at[side], side_send, side_recv,
                tensor=(side + t) % tensors,
            )

    send_take(2)
    send_own(3)
    send_take(3)

    load_left.wait()
    load_right.wait()

    def send_back(s, kind):
        def back(d, carry):
            k = chip_at(d)
            src, owner = (results.at[s, k, core], me) if kind == "own" else (back_take.at[s, k], mate)
            send(
                src, returned.at[owner * slots + s], back_send.at[s], back_recv.at[s],
                fsdp=k * 2 + core,
            )
            return carry

        lax.fori_loop(1, chips, back, 0)

    def wait_back_take(s):
        all_of(back_take.at[s], back_give_send.at[s], back_give_recv.at[s]).wait_recv()
        returned[mate * slots + s] = back_take[s, chip]

    def spread_total():
        @pl.when(chip == speaker)
        def _():
            side_all.wait_recv()
            total[0] = jnp.sum(side_sums[...], axis=0)

            def send_total(d, carry):
                send(total.at[0], total.at[0], total_send, total_recv, fsdp=chip_at(d) * 2 + core)
                return carry

            lax.fori_loop(1, chips, send_total, 0)

    some = returned.at[pl.ds(0, 2 * chips - 2)]
    for s in range(slots):
        all_of(some, go_send.at[s], go_recv.at[s]).wait_recv()
        left_side = jnp.dot(
            lroot[s], arrived[s], preferred_element_type=jnp.float32
        ).astype(jnp.bfloat16)
        product = jnp.dot(left_side, rroot[s], preferred_element_type=jnp.float32)
        results[s] = product.astype(jnp.bfloat16).reshape(chips, 2, rows, size)
        send(
            results.at[s, :, 1 - core], back_take.at[s], back_give_send.at[s], back_give_recv.at[s],
            fsdp=mate,
        )
        returned[me * slots + s] = results[s, chip, core]
        send_back(s, "own")
        if s > 0:
            wait_back_take(s - 1)
            send_back(s - 1, "mate")
        else:
            spread_total()
    wait_back_take(slots - 1)
    send_back(slots - 1, "mate")

    @pl.when(chip != speaker)
    def _():
        all_of(total.at[0], total_send, total_recv).wait_recv()

    grand_sum = jnp.sum(total[0], axis=1, keepdims=True)
    factor = clip_rms / jnp.sqrt(grand_sum / entry_count + eps_norm)
    scale[...] = jnp.broadcast_to(factor, (1, 128))
    lane = lax.broadcasted_iota(jnp.int32, (1, positions), 1)
    gain = []
    for s in range(slots):
        mine = jnp.sum(jnp.where(lane == me * slots + s, filled, 0.0), axis=1, keepdims=True)
        gain.append(factor * factor * mine)
    load_lgram.wait()
    load_rgram.wait()
    for s in range(slots):
        g = arrived[s]
        left_new[s] += gain[s] * lax.dot_general(
            g, g, (((1,), (1,)), ((), ())), preferred_element_type=jnp.float32
        )
        right_new[s] += gain[s] * lax.dot_general(
            g, g, (((0,), (0,)), ((), ())), preferred_element_type=jnp.float32
        )

    for s in range(slots):
        all_of(some, back_send.at[s], back_recv.at[s]).wait_recv()

    @pl.when(chip == speaker)
    def _():
        side_all.wait_send()
        all_of(sums.at[pl.ds(0, chips - 1)], total_send, total_recv).wait_send()

    sum_all.wait_send()
    half.wait_send()
    for s in range(slots):
        all_of(take.at[s], give_send.at[s], give_recv.at[s]).wait_send()
        all_of(take.at[s], back_give_send.at[s], back_give_recv.at[s]).wait_send()
        all_of(some, go_send.at[s], go_recv.at[s]).wait_send()
        all_of(some, back_send.at[s], back_recv.at[s]).wait_send()


def finish_kernel(
    slots, owner_hbm, slot_hbm, left, right, returned, scale, left_new, right_new, update,
    owner, slot, placed, sems, table_sems,
):
    load_owner = pltpu.make_async_copy(owner_hbm, owner, table_sems.at[0])
    load_slot = pltpu.make_async_copy(slot_hbm, slot, table_sems.at[1])
    load_owner.start()
    load_slot.start()
    per_row, row_blocks = owner.shape
    size = left.shape[-1]
    copies = []
    for s in range(slots):
        for ref, new in ((left, left_new), (right, right_new)):
            copies.append(pltpu.make_async_copy(ref.at[s], new.at[s], sems.at[len(copies)]))
            copies[-1].start()

    factor = scale[0:1, 0:1]

    def place(r, carry):
        for c in range(per_row):
            block = returned[owner[c, r] * slots + slot[c, r]].astype(jnp.float32)
            placed[r, :, c * size : (c + 1) * size] = (block * factor).astype(placed.dtype)
        return carry

    load_owner.wait()
    load_slot.wait()
    quarter = row_blocks // 4
    for k in range(0, row_blocks, quarter):
        lax.fori_loop(k, k + quarter, place, 0)
        part = pl.ds(k, quarter)
        copies.append(pltpu.make_async_copy(placed.at[part], update.at[part], sems.at[len(copies)]))
        copies[-1].start()
    for copy in copies:
        copy.wait()


def per_device(gradient, owner, slot, left_gram, right_gram, left_root, right_root):
    row_blocks, rows, col_count = gradient.shape
    slots, size, _ = left_gram.shape
    owners, tensors = lax.axis_size("fsdp"), lax.axis_size("tensor")
    positions, per_row, chips = owners * slots, col_count // size, owners // 2
    entry_count = float(row_blocks * rows * col_count * owners * tensors)
    vmem = pl.BlockSpec(memory_space=pltpu.VMEM)
    dma = pltpu.SemaphoreType.DMA
    bf16, f32, i32 = jnp.bfloat16, jnp.float32, jnp.int32
    hbm = pl.BlockSpec(memory_space=pltpu.HBM)
    owner, slot = owner.T, slot.T
    big = [
        pltpu.with_memory_space_constraint(x, pltpu.HBM)
        for x in (owner, slot, gradient, left_root, right_root, left_gram, right_gram)
    ]
    left, right, returned, scale = pl.pallas_call(
        functools.partial(exchange_kernel, entry_count, owners, tensors, slots, rows, size),
        out_shape=(
            pltpu.VMEM((slots, size, size), f32),
            pltpu.VMEM((slots, size, size), f32),
            pltpu.VMEM((positions, rows, size), bf16),
            pltpu.VMEM((1, 128), f32),
        ),
        in_specs=[hbm] * 7,
        out_specs=(vmem, vmem, vmem, vmem),
        scratch_shapes=[
            pltpu.VMEM((per_row, row_blocks), i32),
            pltpu.VMEM((per_row, row_blocks), i32),
            pltpu.VMEM((row_blocks * per_row, rows, size), f32),
            pltpu.VMEM((slots, size, size), bf16),
            pltpu.VMEM((slots, size, size), bf16),
            pltpu.VMEM((slots, chips, rows, size), bf16),
            pltpu.VMEM((slots, chips, rows, size), bf16),
            pltpu.VMEM((slots, chips, rows, size), bf16),
            pltpu.VMEM((slots, size, size), bf16),
            pltpu.VMEM((slots, chips, 2, rows, size), bf16),
            pltpu.VMEM((slots, chips, rows, size), bf16),
            pltpu.VMEM((1, positions), i32),
            pltpu.SMEM((1, positions), i32),
            pltpu.VMEM((tensors, 1, 128), f32),
            pltpu.VMEM((chips, 1, 128), f32),
            pltpu.VMEM((2, 1, 128), f32),
            pltpu.VMEM((1, 1, 128), f32),
            dma((6 + per_row,)), *[dma] * 9, *[dma((slots,))] * 8,
        ],
        compiler_params=pltpu.CompilerParams(
            collective_id=0, has_side_effects=True, vmem_limit_bytes=32 * 2**20
        ),
        cost_estimate=pl.CostEstimate(
            flops=8 * slots * size**3, bytes_accessed=24 * 2**20, transcendentals=0
        ),
        name="exchange",
    )(*big)
    return pl.pallas_call(
        functools.partial(finish_kernel, slots),
        out_shape=(
            jax.ShapeDtypeStruct(left_gram.shape, f32),
            jax.ShapeDtypeStruct(right_gram.shape, f32),
            jax.ShapeDtypeStruct(gradient.shape, bf16),
        ),
        in_specs=[hbm, hbm, vmem, vmem, vmem, vmem],
        out_specs=(hbm, hbm, hbm),
        scratch_shapes=[
            pltpu.SMEM(owner.shape, i32),
            pltpu.SMEM(owner.shape, i32),
            pltpu.VMEM(gradient.shape, bf16),
            dma((2 * slots + 4,)),
            dma((2,)),
        ],
        compiler_params=pltpu.CompilerParams(vmem_limit_bytes=24 * 2**20),
        cost_estimate=pl.CostEstimate(flops=0, bytes_accessed=9 * 2**20, transcendentals=0),
        name="finish",
    )(*big[:2], left, right, returned, scale)


def solution(mesh):
    return jax.shard_map(
        per_device,
        mesh=mesh,
        in_specs=(
            P(None, "fsdp", "tensor"),
            P(None, "tensor"),
            P(None, "tensor"),
            P(("fsdp", "tensor"), None, None),
            P(("fsdp", "tensor"), None, None),
            P(("fsdp", "tensor"), None, None),
            P(("fsdp", "tensor"), None, None),
        ),
        out_specs=(
            P(("fsdp", "tensor"), None, None),
            P(("fsdp", "tensor"), None, None),
            P(None, "fsdp", "tensor"),
        ),
        check_vma=False,
    )
```

```python
import functools

import jax
import jax.numpy as jnp
from jax import lax
from jax.experimental import pallas as pl
from jax.experimental.pallas import tpu as pltpu
from jax.sharding import PartitionSpec as P

clip_rms = 0.05
eps_norm = 1e-06
MESH = pl.DeviceIdType.MESH


def exchange_kernel(
    entry_count, owners, tensors, slots, rows, size,
    owner_hbm, slot_hbm, grad_hbm, lroot_hbm, rroot_hbm, lgram_hbm, rgram_hbm,
    left_new, right_new, returned, scale,
    owner_ref, slot_ref, grad, lroot, rroot, own, give, take, arrived, results, back_take,
    table_v, table_s, side_sums, sums, halves, total,
    local_sem, table_sem, side_send, side_recv, sum_send, sum_recv, half_send, half_recv, total_send, total_recv,
    give_send, give_recv, go_send, go_recv, back_give_send, back_give_recv, back_send, back_recv,
):
    me = lax.axis_index("fsdp")
    side = lax.axis_index("tensor")
    per_row, row_blocks = owner_ref.shape
    positions = owners * slots
    chips = owners // 2
    chip, core = me // 2, me % 2
    mate = chip * 2 + 1 - core

    barrier = pltpu.get_barrier_semaphore()
    for i in range(1, chips):
        pl.semaphore_signal(
            barrier, inc=1, device_id={"fsdp": (chip + i) % chips * 2 + core}, device_id_type=MESH
        )
    pl.semaphore_signal(barrier, inc=1, device_id={"fsdp": mate}, device_id_type=MESH)

    speaker = 5

    @pl.when(chip == speaker)
    def _():
        for t in range(1, tensors):
            pl.semaphore_signal(
                barrier, inc=1, device_id={"tensor": (side + t) % tensors}, device_id_type=MESH
            )

    load_left = pltpu.make_async_copy(lroot_hbm, lroot, local_sem.at[0])
    load_right = pltpu.make_async_copy(rroot_hbm, rroot, local_sem.at[1])
    load_lgram = pltpu.make_async_copy(lgram_hbm, left_new, local_sem.at[2])
    load_rgram = pltpu.make_async_copy(rgram_hbm, right_new, local_sem.at[3])
    load_grad = [
        pltpu.make_async_copy(
            grad_hbm.at[:, :, pl.ds(c * size, size)],
            grad.at[pl.ds(c * row_blocks, row_blocks)],
            local_sem.at[4 + c],
        )
        for c in range(per_row)
    ]
    load_tables = [
        pltpu.make_async_copy(owner_hbm, owner_ref, local_sem.at[4 + per_row]),
        pltpu.make_async_copy(slot_hbm, slot_ref, local_sem.at[5 + per_row]),
    ]
    for load in load_tables + load_grad:
        load.start()

    for load in load_tables:
        load.wait()
    target = owner_ref[...] * slots + slot_ref[...]
    lanes = lax.broadcasted_iota(jnp.int32, (row_blocks, positions), 1)
    block_rows = lax.broadcasted_iota(jnp.int32, (row_blocks, positions), 0)
    source = jnp.zeros((row_blocks, positions), jnp.int32)
    filled = jnp.zeros((row_blocks, positions), jnp.float32)
    target = target.T
    for c in range(per_row):
        hit = target[:, c : c + 1] == lanes
        source = jnp.where(hit, block_rows + c * row_blocks, source)
        filled = jnp.where(hit, 1.0, filled)
    table_v[...] = jnp.max(source, axis=0, keepdims=True)
    filled = jnp.max(filled, axis=0, keepdims=True)
    load_table = pltpu.make_async_copy(table_v, table_s, table_sem)
    load_table.start()

    for load in load_grad:
        load.wait()
    load_table.wait()
    for load in (load_left, load_right, load_lgram, load_rgram):
        load.start()

    def piece(s, o):
        return grad[table_s[0, o * slots + s]].astype(jnp.bfloat16)

    def rows_of(f):
        return pl.ds(pl.multiple_of(f * rows, rows), rows)

    def chip_at(d):
        d = jnp.where(core == 0, d, 16 - d)
        return (chip // 4 + d // 4) % 4 * 4 + (chip % 4 + d % 4) % 4

    def send(src, dst, send_sem, recv_sem, **to):
        copy = pltpu.make_async_remote_copy(
            src_ref=src, dst_ref=dst, send_sem=send_sem, recv_sem=recv_sem,
            device_id=to, device_id_type=MESH,
        )
        copy.start()
        return copy

    def all_of(some, send_sem, recv_sem):
        return pltpu.make_async_remote_copy(
            src_ref=some, dst_ref=some, send_sem=send_sem, recv_sem=recv_sem,
            device_id={"fsdp": mate}, device_id_type=MESH,
        )

    def fill_give(s):
        def fill(k, carry):
            give[s, k] = piece(s, k * 2 + 1 - core)
            return carry

        lax.fori_loop(0, chips, fill, 0)

    def send_give(s):
        send(give.at[s], take.at[s], give_send.at[s], give_recv.at[s], fsdp=mate)

    def send_own(s):
        def go(d, carry):
            k = chip_at(d)
            o = k * 2 + core
            own[s, k] = piece(s, o)
            send(own.at[s, k], arrived.at[s, rows_of(me), :], go_send.at[s], go_recv.at[s], fsdp=o)
            return carry

        lax.fori_loop(1, chips, go, 0)
        arrived[s, rows_of(me), :] = piece(s, me)

    def send_take(s):
        all_of(take.at[s], give_send.at[s], give_recv.at[s]).wait_recv()

        def go(d, carry):
            k = chip_at(d)
            send(
                take.at[s, k], arrived.at[s, rows_of(mate), :], go_send.at[s], go_recv.at[s],
                fsdp=k * 2 + core,
            )
            return carry

        lax.fori_loop(1, chips, go, 0)
        arrived[s, rows_of(mate), :] = take[s, chip]

    fill_give(0)
    pl.semaphore_wait(barrier, chips + jnp.where(chip == speaker, tensors - 1, 0))

    send_give(0)
    send_own(0)
    fill_give(1)
    send_give(1)

    def square(b, total):
        block = grad[b]
        return total + block * block

    own_sum = lax.fori_loop(0, row_blocks * per_row, square, jnp.zeros((rows, size), jnp.float32))
    own_sum = sum(own_sum[:, k : k + 128] for k in range(0, size, 128))
    sums[chip] = jnp.sum(own_sum, axis=0, keepdims=True)

    def send_sum(d, carry):
        send(sums.at[chip], sums.at[chip], sum_send, sum_recv, fsdp=chip_at(d) * 2 + core)
        return carry

    lax.fori_loop(1, chips, send_sum, 0)
    send_take(0)
    send_own(1)
    fill_give(2)
    send_give(2)
    send_take(1)
    sum_all = all_of(sums.at[pl.ds(0, chips - 1)], sum_send, sum_recv)
    sum_all.wait_recv()
    halves[core] = jnp.sum(sums[...], axis=0)
    half = send(halves.at[core], halves.at[core], half_send, half_recv, fsdp=mate)
    send_own(2)
    fill_give(3)
    send_give(3)
    half.wait_recv()
    side_sums[side] = halves[0] + halves[1]
    side_all = all_of(side_sums.at[pl.ds(0, tensors - 1)], side_send, side_recv)

    @pl.when(chip == speaker)
    def _():
        for t in range(1, tensors):
            send(
                side_sums.at[side], side_sums.at[side], side_send, side_recv,
                tensor=(side + t) % tensors,
            )

    send_take(2)
    send_own(3)
    send_take(3)

    load_left.wait()
    load_right.wait()

    def send_back(s, kind):
        def back(d, carry):
            k = chip_at(d)
            src, owner = (results.at[s, k, core], me) if kind == "own" else (back_take.at[s, k], mate)
            send(
                src, returned.at[owner * slots + s], back_send.at[s], back_recv.at[s],
                fsdp=k * 2 + core,
            )
            return carry

        lax.fori_loop(1, chips, back, 0)

    def wait_back_take(s):
        all_of(back_take.at[s], back_give_send.at[s], back_give_recv.at[s]).wait_recv()
        returned[mate * slots + s] = back_take[s, chip]

    def spread_total():
        @pl.when(chip == speaker)
        def _():
            side_all.wait_recv()
            total[0] = jnp.sum(side_sums[...], axis=0)

            def send_total(d, carry):
                send(total.at[0], total.at[0], total_send, total_recv, fsdp=chip_at(d) * 2 + core)
                return carry

            lax.fori_loop(1, chips, send_total, 0)

    some = returned.at[pl.ds(0, 2 * chips - 2)]
    for s in range(slots):
        all_of(some, go_send.at[s], go_recv.at[s]).wait_recv()
        left_side = jnp.dot(
            lroot[s], arrived[s], preferred_element_type=jnp.float32
        ).astype(jnp.bfloat16)
        product = jnp.dot(left_side, rroot[s], preferred_element_type=jnp.float32)
        results[s] = product.astype(jnp.bfloat16).reshape(chips, 2, rows, size)
        send(
            results.at[s, :, 1 - core], back_take.at[s], back_give_send.at[s], back_give_recv.at[s],
            fsdp=mate,
        )
        returned[me * slots + s] = results[s, chip, core]
        if s > 0:
            wait_back_take(s - 1)
            send_back(s - 1, "mate")
        send_back(s, "own")
        if s == 0:
            spread_total()
    wait_back_take(slots - 1)
    send_back(slots - 1, "mate")

    @pl.when(chip != speaker)
    def _():
        all_of(total.at[0], total_send, total_recv).wait_recv()

    grand_sum = jnp.sum(total[0], axis=1, keepdims=True)
    factor = clip_rms / jnp.sqrt(grand_sum / entry_count + eps_norm)
    scale[...] = jnp.broadcast_to(factor, (1, 128))
    lane = lax.broadcasted_iota(jnp.int32, (1, positions), 1)
    gain = []
    for s in range(slots):
        mine = jnp.sum(jnp.where(lane == me * slots + s, filled, 0.0), axis=1, keepdims=True)
        gain.append(factor * factor * mine)
    load_lgram.wait()
    load_rgram.wait()
    for s in range(slots):
        g = arrived[s]
        left_new[s] += gain[s] * lax.dot_general(
            g, g, (((1,), (1,)), ((), ())), preferred_element_type=jnp.float32
        )
        right_new[s] += gain[s] * lax.dot_general(
            g, g, (((0,), (0,)), ((), ())), preferred_element_type=jnp.float32
        )

    for s in range(slots):
        all_of(some, back_send.at[s], back_recv.at[s]).wait_recv()

    @pl.when(chip == speaker)
    def _():
        side_all.wait_send()
        all_of(sums.at[pl.ds(0, chips - 1)], total_send, total_recv).wait_send()

    sum_all.wait_send()
    half.wait_send()
    for s in range(slots):
        all_of(take.at[s], give_send.at[s], give_recv.at[s]).wait_send()
        all_of(take.at[s], back_give_send.at[s], back_give_recv.at[s]).wait_send()
        all_of(some, go_send.at[s], go_recv.at[s]).wait_send()
        all_of(some, back_send.at[s], back_recv.at[s]).wait_send()


def finish_kernel(
    slots, owner_hbm, slot_hbm, left, right, returned, scale, left_new, right_new, update,
    owner, slot, placed, sems, table_sems,
):
    load_owner = pltpu.make_async_copy(owner_hbm, owner, table_sems.at[0])
    load_slot = pltpu.make_async_copy(slot_hbm, slot, table_sems.at[1])
    load_owner.start()
    load_slot.start()
    per_row, row_blocks = owner.shape
    size = left.shape[-1]
    copies = []
    for s in range(slots):
        for ref, new in ((left, left_new), (right, right_new)):
            copies.append(pltpu.make_async_copy(ref.at[s], new.at[s], sems.at[len(copies)]))
            copies[-1].start()

    factor = scale[0:1, 0:1]

    def place(r, carry):
        for c in range(per_row):
            block = returned[owner[c, r] * slots + slot[c, r]].astype(jnp.float32)
            placed[r, :, c * size : (c + 1) * size] = (block * factor).astype(placed.dtype)
        return carry

    load_owner.wait()
    load_slot.wait()
    quarter = row_blocks // 4
    for k in range(0, row_blocks, quarter):
        lax.fori_loop(k, k + quarter, place, 0)
        part = pl.ds(k, quarter)
        copies.append(pltpu.make_async_copy(placed.at[part], update.at[part], sems.at[len(copies)]))
        copies[-1].start()
    for copy in copies:
        copy.wait()


def per_device(gradient, owner, slot, left_gram, right_gram, left_root, right_root):
    row_blocks, rows, col_count = gradient.shape
    slots, size, _ = left_gram.shape
    owners, tensors = lax.axis_size("fsdp"), lax.axis_size("tensor")
    positions, per_row, chips = owners * slots, col_count // size, owners // 2
    entry_count = float(row_blocks * rows * col_count * owners * tensors)
    vmem = pl.BlockSpec(memory_space=pltpu.VMEM)
    dma = pltpu.SemaphoreType.DMA
    bf16, f32, i32 = jnp.bfloat16, jnp.float32, jnp.int32
    hbm = pl.BlockSpec(memory_space=pltpu.HBM)
    owner, slot = owner.T, slot.T
    big = [
        pltpu.with_memory_space_constraint(x, pltpu.HBM)
        for x in (owner, slot, gradient, left_root, right_root, left_gram, right_gram)
    ]
    left, right, returned, scale = pl.pallas_call(
        functools.partial(exchange_kernel, entry_count, owners, tensors, slots, rows, size),
        out_shape=(
            pltpu.VMEM((slots, size, size), f32),
            pltpu.VMEM((slots, size, size), f32),
            pltpu.VMEM((positions, rows, size), bf16),
            pltpu.VMEM((1, 128), f32),
        ),
        in_specs=[hbm] * 7,
        out_specs=(vmem, vmem, vmem, vmem),
        scratch_shapes=[
            pltpu.VMEM((per_row, row_blocks), i32),
            pltpu.VMEM((per_row, row_blocks), i32),
            pltpu.VMEM((row_blocks * per_row, rows, size), f32),
            pltpu.VMEM((slots, size, size), bf16),
            pltpu.VMEM((slots, size, size), bf16),
            pltpu.VMEM((slots, chips, rows, size), bf16),
            pltpu.VMEM((slots, chips, rows, size), bf16),
            pltpu.VMEM((slots, chips, rows, size), bf16),
            pltpu.VMEM((slots, size, size), bf16),
            pltpu.VMEM((slots, chips, 2, rows, size), bf16),
            pltpu.VMEM((slots, chips, rows, size), bf16),
            pltpu.VMEM((1, positions), i32),
            pltpu.SMEM((1, positions), i32),
            pltpu.VMEM((tensors, 1, 128), f32),
            pltpu.VMEM((chips, 1, 128), f32),
            pltpu.VMEM((2, 1, 128), f32),
            pltpu.VMEM((1, 1, 128), f32),
            dma((6 + per_row,)), *[dma] * 9, *[dma((slots,))] * 8,
        ],
        compiler_params=pltpu.CompilerParams(
            collective_id=0, has_side_effects=True, vmem_limit_bytes=32 * 2**20
        ),
        cost_estimate=pl.CostEstimate(
            flops=8 * slots * size**3, bytes_accessed=24 * 2**20, transcendentals=0
        ),
        name="exchange",
    )(*big)
    return pl.pallas_call(
        functools.partial(finish_kernel, slots),
        out_shape=(
            jax.ShapeDtypeStruct(left_gram.shape, f32),
            jax.ShapeDtypeStruct(right_gram.shape, f32),
            jax.ShapeDtypeStruct(gradient.shape, bf16),
        ),
        in_specs=[hbm, hbm, vmem, vmem, vmem, vmem],
        out_specs=(hbm, hbm, hbm),
        scratch_shapes=[
            pltpu.SMEM(owner.shape, i32),
            pltpu.SMEM(owner.shape, i32),
            pltpu.VMEM(gradient.shape, bf16),
            dma((2 * slots + 4,)),
            dma((2,)),
        ],
        compiler_params=pltpu.CompilerParams(vmem_limit_bytes=24 * 2**20),
        cost_estimate=pl.CostEstimate(flops=0, bytes_accessed=9 * 2**20, transcendentals=0),
        name="finish",
    )(*big[:2], left, right, returned, scale)


def solution(mesh):
    return jax.shard_map(
        per_device,
        mesh=mesh,
        in_specs=(
            P(None, "fsdp", "tensor"),
            P(None, "tensor"),
            P(None, "tensor"),
            P(("fsdp", "tensor"), None, None),
            P(("fsdp", "tensor"), None, None),
            P(("fsdp", "tensor"), None, None),
            P(("fsdp", "tensor"), None, None),
        ),
        out_specs=(
            P(("fsdp", "tensor"), None, None),
            P(("fsdp", "tensor"), None, None),
            P(None, "fsdp", "tensor"),
        ),
        check_vma=False,
    )
```

```python
import functools

import jax
import jax.numpy as jnp
from jax import lax
from jax.experimental import pallas as pl
from jax.experimental.pallas import tpu as pltpu
from jax.sharding import PartitionSpec as P

clip_rms = 0.05
eps_norm = 1e-06
MESH = pl.DeviceIdType.MESH


def exchange_kernel(
    entry_count, owners, tensors, slots, rows, size,
    owner_hbm, slot_hbm, grad_hbm, lroot_hbm, rroot_hbm, lgram_hbm, rgram_hbm,
    left_new, right_new, returned, scale,
    owner_ref, slot_ref, grad, lroot, rroot, box, give, arrived, results, back_take,
    table_v, table_s, side_sums, sums, halves, total,
    local_sem, table_sem, side_send, side_recv, sum_send, sum_recv, half_send, half_recv, total_send, total_recv,
    give_send, give_recv, go_send, go_recv, back_give_send, back_give_recv, back_send, back_recv,
):
    me = lax.axis_index("fsdp")
    side = lax.axis_index("tensor")
    per_row, row_blocks = owner_ref.shape
    positions = owners * slots
    chips = owners // 2
    chip, core = me // 2, me % 2
    mate = chip * 2 + 1 - core

    barrier = pltpu.get_barrier_semaphore()
    for i in range(1, chips):
        pl.semaphore_signal(
            barrier, inc=1, device_id={"fsdp": (chip + i) % chips * 2 + core}, device_id_type=MESH
        )
    pl.semaphore_signal(barrier, inc=1, device_id={"fsdp": mate}, device_id_type=MESH)

    speaker = 5

    @pl.when(chip == speaker)
    def _():
        for t in range(1, tensors):
            pl.semaphore_signal(
                barrier, inc=1, device_id={"tensor": (side + t) % tensors}, device_id_type=MESH
            )

    load_left = pltpu.make_async_copy(lroot_hbm, lroot, local_sem.at[0])
    load_right = pltpu.make_async_copy(rroot_hbm, rroot, local_sem.at[1])
    load_lgram = pltpu.make_async_copy(lgram_hbm, left_new, local_sem.at[2])
    load_rgram = pltpu.make_async_copy(rgram_hbm, right_new, local_sem.at[3])
    load_grad = [
        pltpu.make_async_copy(
            grad_hbm.at[:, :, pl.ds(c * size, size)],
            grad.at[pl.ds(c * row_blocks, row_blocks)],
            local_sem.at[4 + c],
        )
        for c in range(per_row)
    ]
    load_tables = [
        pltpu.make_async_copy(owner_hbm, owner_ref, local_sem.at[4 + per_row]),
        pltpu.make_async_copy(slot_hbm, slot_ref, local_sem.at[5 + per_row]),
    ]
    for load in load_tables + load_grad:
        load.start()

    for load in load_tables:
        load.wait()
    target = owner_ref[...] * slots + slot_ref[...]
    lanes = lax.broadcasted_iota(jnp.int32, (row_blocks, positions), 1)
    block_rows = lax.broadcasted_iota(jnp.int32, (row_blocks, positions), 0)
    source = jnp.zeros((row_blocks, positions), jnp.int32)
    filled = jnp.zeros((row_blocks, positions), jnp.float32)
    target = target.T
    for c in range(per_row):
        hit = target[:, c : c + 1] == lanes
        source = jnp.where(hit, block_rows + c * row_blocks, source)
        filled = jnp.where(hit, 1.0, filled)
    table_v[...] = jnp.max(source, axis=0, keepdims=True)
    filled = jnp.max(filled, axis=0, keepdims=True)
    load_table = pltpu.make_async_copy(table_v, table_s, table_sem)
    load_table.start()

    for load in load_grad:
        load.wait()
    load_table.wait()
    for load in (load_left, load_right, load_lgram, load_rgram):
        load.start()

    def piece(s, o):
        return grad[table_s[0, o * slots + s]].astype(jnp.bfloat16)

    def rows_of(f):
        return pl.ds(pl.multiple_of(f * rows, rows), rows)

    def chip_at(d):
        return (chip // 4 + d // 4) % 4 * 4 + (chip % 4 + d % 4) % 4

    def send(src, dst, send_sem, recv_sem, **to):
        copy = pltpu.make_async_remote_copy(
            src_ref=src, dst_ref=dst, send_sem=send_sem, recv_sem=recv_sem,
            device_id=to, device_id_type=MESH,
        )
        copy.start()
        return copy

    def all_of(some, send_sem, recv_sem):
        return pltpu.make_async_remote_copy(
            src_ref=some, dst_ref=some, send_sem=send_sem, recv_sem=recv_sem,
            device_id={"fsdp": mate}, device_id_type=MESH,
        )

    def fill_give(s):
        def fill(k, carry):
            give[s, k] = piece(s, k * 2 + 1 - core)
            return carry

        lax.fori_loop(0, chips, fill, 0)

    def send_give(s):
        send(give.at[s], box.at[s, :, core], give_send.at[s], give_recv.at[s], fsdp=mate)

    def fill_own(s):
        def fill(k, carry):
            box[s, k, core] = piece(s, k * 2 + core)
            return carry

        lax.fori_loop(0, chips, fill, 0)

    def send_half(s, half, source):
        def go(d, carry):
            k = chip_at(d)
            send(
                box.at[s, k, half], arrived.at[s, source], go_send.at[s], go_recv.at[s],
                fsdp=k * 2 + core,
            )
            return carry

        lax.fori_loop(1, chips, go, 0)
        arrived[s, source] = box[s, chip, half]

    def wait_give(s):
        all_of(give.at[s], give_send.at[s], give_recv.at[s]).wait_recv()

    def send_box(s):
        wait_give(s)
        pair = pl.ds(chip * 2, 2)

        def go(d, carry):
            k = chip_at(d)
            send(
                box.at[s, k], arrived.at[s, pair], go_send.at[s], go_recv.at[s], fsdp=k * 2 + core
            )
            return carry

        lax.fori_loop(1, chips, go, 0)
        arrived[s, pair] = box[s, chip]

    fill_give(0)
    pl.semaphore_wait(barrier, chips + jnp.where(chip == speaker, tensors - 1, 0))

    send_give(0)
    fill_own(0)
    send_half(0, core, me)
    fill_give(1)
    send_give(1)

    def square(b, total):
        block = grad[b]
        return total + block * block

    own_sum = lax.fori_loop(0, row_blocks * per_row, square, jnp.zeros((rows, size), jnp.float32))
    own_sum = sum(own_sum[:, k : k + 128] for k in range(0, size, 128))
    sums[chip] = jnp.sum(own_sum, axis=0, keepdims=True)

    def send_sum(d, carry):
        send(sums.at[chip], sums.at[chip], sum_send, sum_recv, fsdp=chip_at(d) * 2 + core)
        return carry

    lax.fori_loop(1, chips, send_sum, 0)
    wait_give(0)
    send_half(0, 1 - core, mate)
    fill_own(1)
    fill_give(2)
    send_give(2)
    send_box(1)
    sum_all = all_of(sums.at[pl.ds(0, chips - 1)], sum_send, sum_recv)
    sum_all.wait_recv()
    halves[core] = jnp.sum(sums[...], axis=0)
    half = send(halves.at[core], halves.at[core], half_send, half_recv, fsdp=mate)
    fill_own(2)
    fill_give(3)
    send_give(3)
    send_box(2)
    half.wait_recv()
    side_sums[side] = halves[0] + halves[1]
    side_all = all_of(side_sums.at[pl.ds(0, tensors - 1)], side_send, side_recv)

    @pl.when(chip == speaker)
    def _():
        for t in range(1, tensors):
            send(
                side_sums.at[side], side_sums.at[side], side_send, side_recv,
                tensor=(side + t) % tensors,
            )

    fill_own(3)
    send_box(3)

    load_left.wait()
    load_right.wait()

    def send_back(s, kind):
        def back(d, carry):
            k = chip_at(d)
            src, owner = (results.at[s, k, core], me) if kind == "own" else (back_take.at[s, k], mate)
            send(
                src, returned.at[owner * slots + s], back_send.at[s], back_recv.at[s],
                fsdp=k * 2 + core,
            )
            return carry

        lax.fori_loop(1, chips, back, 0)

    def wait_back_take(s):
        all_of(back_take.at[s], back_give_send.at[s], back_give_recv.at[s]).wait_recv()
        returned[mate * slots + s] = back_take[s, chip]

    def spread_total():
        @pl.when(chip == speaker)
        def _():
            side_all.wait_recv()
            total[0] = jnp.sum(side_sums[...], axis=0)

            def send_total(d, carry):
                send(total.at[0], total.at[0], total_send, total_recv, fsdp=chip_at(d) * 2 + core)
                return carry

            lax.fori_loop(1, chips, send_total, 0)

    some = returned.at[pl.ds(0, 2 * chips - 2)]
    for s in range(slots):
        all_of(some, go_send.at[s], go_recv.at[s]).wait_recv()
        left_side = jnp.dot(
            lroot[s], arrived[s].reshape(size, size), preferred_element_type=jnp.float32
        ).astype(jnp.bfloat16)
        product = jnp.dot(left_side, rroot[s], preferred_element_type=jnp.float32)
        results[s] = product.astype(jnp.bfloat16).reshape(chips, 2, rows, size)
        send(
            results.at[s, :, 1 - core], back_take.at[s], back_give_send.at[s], back_give_recv.at[s],
            fsdp=mate,
        )
        returned[me * slots + s] = results[s, chip, core]
        send_back(s, "own")
        if s > 0:
            wait_back_take(s - 1)
            send_back(s - 1, "mate")
        else:
            spread_total()
    wait_back_take(slots - 1)
    send_back(slots - 1, "mate")

    @pl.when(chip != speaker)
    def _():
        all_of(total.at[0], total_send, total_recv).wait_recv()

    grand_sum = jnp.sum(total[0], axis=1, keepdims=True)
    factor = clip_rms / jnp.sqrt(grand_sum / entry_count + eps_norm)
    scale[...] = jnp.broadcast_to(factor, (1, 128))
    lane = lax.broadcasted_iota(jnp.int32, (1, positions), 1)
    gain = []
    for s in range(slots):
        mine = jnp.sum(jnp.where(lane == me * slots + s, filled, 0.0), axis=1, keepdims=True)
        gain.append(factor * factor * mine)
    load_lgram.wait()
    load_rgram.wait()
    for s in range(slots):
        g = arrived[s].reshape(size, size)
        left_new[s] += gain[s] * lax.dot_general(
            g, g, (((1,), (1,)), ((), ())), preferred_element_type=jnp.float32
        )
        right_new[s] += gain[s] * lax.dot_general(
            g, g, (((0,), (0,)), ((), ())), preferred_element_type=jnp.float32
        )

    for s in range(slots):
        all_of(some, back_send.at[s], back_recv.at[s]).wait_recv()

    @pl.when(chip == speaker)
    def _():
        side_all.wait_send()
        all_of(sums.at[pl.ds(0, chips - 1)], total_send, total_recv).wait_send()

    sum_all.wait_send()
    half.wait_send()
    for s in range(slots):
        all_of(give.at[s], give_send.at[s], give_recv.at[s]).wait_send()
        all_of(give.at[s], back_give_send.at[s], back_give_recv.at[s]).wait_send()
        all_of(some, go_send.at[s], go_recv.at[s]).wait_send()
        all_of(some, back_send.at[s], back_recv.at[s]).wait_send()


def finish_kernel(
    slots, owner_hbm, slot_hbm, left, right, returned, scale, left_new, right_new, update,
    owner, slot, placed, sems, table_sems,
):
    load_owner = pltpu.make_async_copy(owner_hbm, owner, table_sems.at[0])
    load_slot = pltpu.make_async_copy(slot_hbm, slot, table_sems.at[1])
    load_owner.start()
    load_slot.start()
    per_row, row_blocks = owner.shape
    size = left.shape[-1]
    copies = []
    for s in range(slots):
        for ref, new in ((left, left_new), (right, right_new)):
            copies.append(pltpu.make_async_copy(ref.at[s], new.at[s], sems.at[len(copies)]))
            copies[-1].start()

    factor = scale[0:1, 0:1]

    def place(r, carry):
        for c in range(per_row):
            block = returned[owner[c, r] * slots + slot[c, r]].astype(jnp.float32)
            placed[r, :, c * size : (c + 1) * size] = (block * factor).astype(placed.dtype)
        return carry

    load_owner.wait()
    load_slot.wait()
    quarter = row_blocks // 4
    for k in range(0, row_blocks, quarter):
        lax.fori_loop(k, k + quarter, place, 0)
        part = pl.ds(k, quarter)
        copies.append(pltpu.make_async_copy(placed.at[part], update.at[part], sems.at[len(copies)]))
        copies[-1].start()
    for copy in copies:
        copy.wait()


def per_device(gradient, owner, slot, left_gram, right_gram, left_root, right_root):
    row_blocks, rows, col_count = gradient.shape
    slots, size, _ = left_gram.shape
    owners, tensors = lax.axis_size("fsdp"), lax.axis_size("tensor")
    positions, per_row, chips = owners * slots, col_count // size, owners // 2
    entry_count = float(row_blocks * rows * col_count * owners * tensors)
    vmem = pl.BlockSpec(memory_space=pltpu.VMEM)
    dma = pltpu.SemaphoreType.DMA
    bf16, f32, i32 = jnp.bfloat16, jnp.float32, jnp.int32
    hbm = pl.BlockSpec(memory_space=pltpu.HBM)
    owner, slot = owner.T, slot.T
    big = [
        pltpu.with_memory_space_constraint(x, pltpu.HBM)
        for x in (owner, slot, gradient, left_root, right_root, left_gram, right_gram)
    ]
    left, right, returned, scale = pl.pallas_call(
        functools.partial(exchange_kernel, entry_count, owners, tensors, slots, rows, size),
        out_shape=(
            pltpu.VMEM((slots, size, size), f32),
            pltpu.VMEM((slots, size, size), f32),
            pltpu.VMEM((positions, rows, size), bf16),
            pltpu.VMEM((1, 128), f32),
        ),
        in_specs=[hbm] * 7,
        out_specs=(vmem, vmem, vmem, vmem),
        scratch_shapes=[
            pltpu.VMEM((per_row, row_blocks), i32),
            pltpu.VMEM((per_row, row_blocks), i32),
            pltpu.VMEM((row_blocks * per_row, rows, size), f32),
            pltpu.VMEM((slots, size, size), bf16),
            pltpu.VMEM((slots, size, size), bf16),
            pltpu.VMEM((slots, chips, 2, rows, size), bf16),
            pltpu.VMEM((slots, chips, rows, size), bf16),
            pltpu.VMEM((slots, owners, rows, size), bf16),
            pltpu.VMEM((slots, chips, 2, rows, size), bf16),
            pltpu.VMEM((slots, chips, rows, size), bf16),
            pltpu.VMEM((1, positions), i32),
            pltpu.SMEM((1, positions), i32),
            pltpu.VMEM((tensors, 1, 128), f32),
            pltpu.VMEM((chips, 1, 128), f32),
            pltpu.VMEM((2, 1, 128), f32),
            pltpu.VMEM((1, 1, 128), f32),
            dma((6 + per_row,)), *[dma] * 9, *[dma((slots,))] * 8,
        ],
        compiler_params=pltpu.CompilerParams(
            collective_id=0, has_side_effects=True, vmem_limit_bytes=32 * 2**20
        ),
        cost_estimate=pl.CostEstimate(
            flops=8 * slots * size**3, bytes_accessed=24 * 2**20, transcendentals=0
        ),
        name="exchange",
    )(*big)
    return pl.pallas_call(
        functools.partial(finish_kernel, slots),
        out_shape=(
            jax.ShapeDtypeStruct(left_gram.shape, f32),
            jax.ShapeDtypeStruct(right_gram.shape, f32),
            jax.ShapeDtypeStruct(gradient.shape, bf16),
        ),
        in_specs=[hbm, hbm, vmem, vmem, vmem, vmem],
        out_specs=(hbm, hbm, hbm),
        scratch_shapes=[
            pltpu.SMEM(owner.shape, i32),
            pltpu.SMEM(owner.shape, i32),
            pltpu.VMEM(gradient.shape, bf16),
            dma((2 * slots + 4,)),
            dma((2,)),
        ],
        compiler_params=pltpu.CompilerParams(vmem_limit_bytes=24 * 2**20),
        cost_estimate=pl.CostEstimate(flops=0, bytes_accessed=9 * 2**20, transcendentals=0),
        name="finish",
    )(*big[:2], left, right, returned, scale)


def solution(mesh):
    return jax.shard_map(
        per_device,
        mesh=mesh,
        in_specs=(
            P(None, "fsdp", "tensor"),
            P(None, "tensor"),
            P(None, "tensor"),
            P(("fsdp", "tensor"), None, None),
            P(("fsdp", "tensor"), None, None),
            P(("fsdp", "tensor"), None, None),
            P(("fsdp", "tensor"), None, None),
        ),
        out_specs=(
            P(("fsdp", "tensor"), None, None),
            P(("fsdp", "tensor"), None, None),
            P(None, "fsdp", "tensor"),
        ),
        check_vma=False,
    )
```

```python
import functools

import jax
import jax.numpy as jnp
from jax import lax
from jax.experimental import pallas as pl
from jax.experimental.pallas import tpu as pltpu
from jax.sharding import PartitionSpec as P

clip_rms = 0.05
eps_norm = 1e-06
MESH = pl.DeviceIdType.MESH


def exchange_kernel(
    entry_count, owners, tensors, slots, rows, size,
    owner_hbm, slot_hbm, grad_hbm, lroot_hbm, rroot_hbm, lgram_hbm, rgram_hbm,
    left_new, right_new, returned, scale,
    owner_ref, slot_ref, grad, lroot, rroot, own, give, take, arrived, results, back_take,
    table_v, table_s, side_sums, sums, halves, total,
    local_sem, table_sem, side_send, side_recv, sum_send, sum_recv, half_send, half_recv, total_send, total_recv,
    give_send, give_recv, go_send, go_recv, back_give_send, back_give_recv, back_send, back_recv,
):
    me = lax.axis_index("fsdp")
    side = lax.axis_index("tensor")
    per_row, row_blocks = owner_ref.shape
    positions = owners * slots
    chips = owners // 2
    chip, core = me // 2, me % 2
    mate = chip * 2 + 1 - core

    load_left = pltpu.make_async_copy(lroot_hbm, lroot, local_sem.at[0])
    load_right = pltpu.make_async_copy(rroot_hbm, rroot, local_sem.at[1])
    load_lgram = pltpu.make_async_copy(lgram_hbm, left_new, local_sem.at[2])
    load_rgram = pltpu.make_async_copy(rgram_hbm, right_new, local_sem.at[3])
    load_grad = [
        pltpu.make_async_copy(
            grad_hbm.at[:, :, pl.ds(c * size, size)],
            grad.at[pl.ds(c * row_blocks, row_blocks)],
            local_sem.at[4 + c],
        )
        for c in range(per_row)
    ]
    load_tables = [
        pltpu.make_async_copy(owner_hbm, owner_ref, local_sem.at[4 + per_row]),
        pltpu.make_async_copy(slot_hbm, slot_ref, local_sem.at[5 + per_row]),
    ]
    for load in load_tables:
        load.start()

    barrier = pltpu.get_barrier_semaphore()
    for i in range(1, chips):
        pl.semaphore_signal(
            barrier, inc=1, device_id={"fsdp": (chip + i) % chips * 2 + core}, device_id_type=MESH
        )
    pl.semaphore_signal(barrier, inc=1, device_id={"fsdp": mate}, device_id_type=MESH)

    speaker = 5

    @pl.when(chip == speaker)
    def _():
        for t in range(1, tensors):
            pl.semaphore_signal(
                barrier, inc=1, device_id={"tensor": (side + t) % tensors}, device_id_type=MESH
            )

    for load in load_grad:
        load.start()

    for load in load_tables:
        load.wait()
    target = owner_ref[...] * slots + slot_ref[...]
    lanes = lax.broadcasted_iota(jnp.int32, (row_blocks, positions), 1)
    block_rows = lax.broadcasted_iota(jnp.int32, (row_blocks, positions), 0)
    source = jnp.zeros((row_blocks, positions), jnp.int32)
    filled = jnp.zeros((row_blocks, positions), jnp.float32)
    target = target.T
    for c in range(per_row):
        hit = target[:, c : c + 1] == lanes
        source = jnp.where(hit, block_rows + c * row_blocks, source)
        filled = jnp.where(hit, 1.0, filled)
    table_v[...] = jnp.max(source, axis=0, keepdims=True)
    filled = jnp.max(filled, axis=0, keepdims=True)
    load_table = pltpu.make_async_copy(table_v, table_s, table_sem)
    load_table.start()

    for load in load_grad:
        load.wait()
    load_table.wait()
    for load in (load_left, load_right, load_lgram, load_rgram):
        load.start()

    def piece(s, o):
        return grad[table_s[0, o * slots + s]].astype(jnp.bfloat16)

    def rows_of(f):
        return pl.ds(pl.multiple_of(f * rows, rows), rows)

    def chip_at(d):
        return (chip // 4 + d // 4) % 4 * 4 + (chip % 4 + d % 4) % 4

    def send(src, dst, send_sem, recv_sem, **to):
        copy = pltpu.make_async_remote_copy(
            src_ref=src, dst_ref=dst, send_sem=send_sem, recv_sem=recv_sem,
            device_id=to, device_id_type=MESH,
        )
        copy.start()
        return copy

    def all_of(some, send_sem, recv_sem):
        return pltpu.make_async_remote_copy(
            src_ref=some, dst_ref=some, send_sem=send_sem, recv_sem=recv_sem,
            device_id={"fsdp": mate}, device_id_type=MESH,
        )

    def fill_give(s):
        def fill(k, carry):
            give[s, k] = piece(s, k * 2 + 1 - core)
            return carry

        lax.fori_loop(0, chips, fill, 0, unroll=True)

    def send_give(s):
        send(give.at[s], take.at[s], give_send.at[s], give_recv.at[s], fsdp=mate)

    def send_own(s):
        def go(d, carry):
            k = chip_at(d)
            o = k * 2 + core
            own[s, k] = piece(s, o)
            send(own.at[s, k], arrived.at[s, rows_of(me), :], go_send.at[s], go_recv.at[s], fsdp=o)
            return carry

        lax.fori_loop(1, chips, go, 0, unroll=True)
        arrived[s, rows_of(me), :] = piece(s, me)

    def send_take(s):
        all_of(take.at[s], give_send.at[s], give_recv.at[s]).wait_recv()

        def go(d, carry):
            k = chip_at(d)
            send(
                take.at[s, k], arrived.at[s, rows_of(mate), :], go_send.at[s], go_recv.at[s],
                fsdp=k * 2 + core,
            )
            return carry

        lax.fori_loop(1, chips, go, 0)
        arrived[s, rows_of(mate), :] = take[s, chip]

    fill_give(0)
    pl.semaphore_wait(barrier, chips + jnp.where(chip == speaker, tensors - 1, 0))

    send_give(0)
    send_own(0)
    fill_give(1)
    send_give(1)

    def square(b, total):
        block = grad[b]
        return total + block * block

    own_sum = lax.fori_loop(0, row_blocks * per_row, square, jnp.zeros((rows, size), jnp.float32))
    own_sum = sum(own_sum[:, k : k + 128] for k in range(0, size, 128))
    sums[chip] = jnp.sum(own_sum, axis=0, keepdims=True)

    def send_sum(d, carry):
        send(sums.at[chip], sums.at[chip], sum_send, sum_recv, fsdp=chip_at(d) * 2 + core)
        return carry

    lax.fori_loop(1, chips, send_sum, 0)
    send_take(0)
    send_own(1)
    fill_give(2)
    send_give(2)
    send_take(1)
    sum_all = all_of(sums.at[pl.ds(0, chips - 1)], sum_send, sum_recv)
    sum_all.wait_recv()
    halves[core] = jnp.sum(sums[...], axis=0)
    half = send(halves.at[core], halves.at[core], half_send, half_recv, fsdp=mate)
    send_own(2)
    fill_give(3)
    send_give(3)
    half.wait_recv()
    side_sums[side] = halves[0] + halves[1]
    side_all = all_of(side_sums.at[pl.ds(0, tensors - 1)], side_send, side_recv)

    @pl.when(chip == speaker)
    def _():
        for t in range(1, tensors):
            send(
                side_sums.at[side], side_sums.at[side], side_send, side_recv,
                tensor=(side + t) % tensors,
            )

    send_take(2)
    send_own(3)
    send_take(3)

    load_left.wait()
    load_right.wait()

    def send_back(s, kind):
        def back(d, carry):
            k = chip_at(d)
            src, owner = (results.at[s, k, core], me) if kind == "own" else (back_take.at[s, k], mate)
            send(
                src, returned.at[owner * slots + s], back_send.at[s], back_recv.at[s],
                fsdp=k * 2 + core,
            )
            return carry

        lax.fori_loop(1, chips, back, 0)

    def wait_back_take(s):
        all_of(back_take.at[s], back_give_send.at[s], back_give_recv.at[s]).wait_recv()
        returned[mate * slots + s] = back_take[s, chip]

    def spread_total():
        @pl.when(chip == speaker)
        def _():
            side_all.wait_recv()
            total[0] = jnp.sum(side_sums[...], axis=0)

            def send_total(d, carry):
                send(total.at[0], total.at[0], total_send, total_recv, fsdp=chip_at(d) * 2 + core)
                return carry

            lax.fori_loop(1, chips, send_total, 0)

    some = returned.at[pl.ds(0, 2 * chips - 2)]
    for s in range(slots):
        all_of(some, go_send.at[s], go_recv.at[s]).wait_recv()
        left_side = jnp.dot(
            lroot[s], arrived[s], preferred_element_type=jnp.float32
        ).astype(jnp.bfloat16)
        product = jnp.dot(left_side, rroot[s], preferred_element_type=jnp.float32)
        results[s] = product.astype(jnp.bfloat16).reshape(chips, 2, rows, size)
        send(
            results.at[s, :, 1 - core], back_take.at[s], back_give_send.at[s], back_give_recv.at[s],
            fsdp=mate,
        )
        returned[me * slots + s] = results[s, chip, core]
        if s > 0:
            wait_back_take(s - 1)
            send_back(s - 1, "mate")
        send_back(s, "own")
        if s == 0:
            spread_total()
    wait_back_take(slots - 1)
    send_back(slots - 1, "mate")

    @pl.when(chip != speaker)
    def _():
        all_of(total.at[0], total_send, total_recv).wait_recv()

    grand_sum = jnp.sum(total[0], axis=1, keepdims=True)
    factor = clip_rms / jnp.sqrt(grand_sum / entry_count + eps_norm)
    scale[...] = jnp.broadcast_to(factor, (1, 128))
    lane = lax.broadcasted_iota(jnp.int32, (1, positions), 1)
    gain = []
    for s in range(slots):
        mine = jnp.sum(jnp.where(lane == me * slots + s, filled, 0.0), axis=1, keepdims=True)
        gain.append(factor * factor * mine)
    load_lgram.wait()
    load_rgram.wait()
    for s in range(slots):
        g = arrived[s]
        left_new[s] += gain[s] * lax.dot_general(
            g, g, (((1,), (1,)), ((), ())), preferred_element_type=jnp.float32
        )
        right_new[s] += gain[s] * lax.dot_general(
            g, g, (((0,), (0,)), ((), ())), preferred_element_type=jnp.float32
        )

    for s in range(slots):
        all_of(some, back_send.at[s], back_recv.at[s]).wait_recv()

    @pl.when(chip == speaker)
    def _():
        side_all.wait_send()
        all_of(sums.at[pl.ds(0, chips - 1)], total_send, total_recv).wait_send()

    sum_all.wait_send()
    half.wait_send()
    for s in range(slots):
        all_of(take.at[s], give_send.at[s], give_recv.at[s]).wait_send()
        all_of(take.at[s], back_give_send.at[s], back_give_recv.at[s]).wait_send()
        all_of(some, go_send.at[s], go_recv.at[s]).wait_send()
        all_of(some, back_send.at[s], back_recv.at[s]).wait_send()


def finish_kernel(
    slots, owner_hbm, slot_hbm, left, right, returned, scale, left_new, right_new, update,
    owner, slot, placed, sems, table_sems,
):
    load_owner = pltpu.make_async_copy(owner_hbm, owner, table_sems.at[0])
    load_slot = pltpu.make_async_copy(slot_hbm, slot, table_sems.at[1])
    load_owner.start()
    load_slot.start()
    per_row, row_blocks = owner.shape
    size = left.shape[-1]
    copies = []
    for s in range(slots):
        for ref, new in ((left, left_new), (right, right_new)):
            copies.append(pltpu.make_async_copy(ref.at[s], new.at[s], sems.at[len(copies)]))
            copies[-1].start()

    factor = scale[0:1, 0:1]

    def place(r, carry):
        for c in range(per_row):
            block = returned[owner[c, r] * slots + slot[c, r]].astype(jnp.float32)
            placed[r, :, c * size : (c + 1) * size] = (block * factor).astype(placed.dtype)
        return carry

    load_owner.wait()
    load_slot.wait()
    quarter = row_blocks // 4
    for k in range(0, row_blocks, quarter):
        lax.fori_loop(k, k + quarter, place, 0)
        part = pl.ds(k, quarter)
        copies.append(pltpu.make_async_copy(placed.at[part], update.at[part], sems.at[len(copies)]))
        copies[-1].start()
    for copy in copies:
        copy.wait()


def per_device(gradient, owner, slot, left_gram, right_gram, left_root, right_root):
    row_blocks, rows, col_count = gradient.shape
    slots, size, _ = left_gram.shape
    owners, tensors = lax.axis_size("fsdp"), lax.axis_size("tensor")
    positions, per_row, chips = owners * slots, col_count // size, owners // 2
    entry_count = float(row_blocks * rows * col_count * owners * tensors)
    vmem = pl.BlockSpec(memory_space=pltpu.VMEM)
    dma = pltpu.SemaphoreType.DMA
    bf16, f32, i32 = jnp.bfloat16, jnp.float32, jnp.int32
    hbm = pl.BlockSpec(memory_space=pltpu.HBM)
    owner, slot = owner.T, slot.T
    big = [
        pltpu.with_memory_space_constraint(x, pltpu.HBM)
        for x in (owner, slot, gradient, left_root, right_root, left_gram, right_gram)
    ]
    left, right, returned, scale = pl.pallas_call(
        functools.partial(exchange_kernel, entry_count, owners, tensors, slots, rows, size),
        out_shape=(
            pltpu.VMEM((slots, size, size), f32),
            pltpu.VMEM((slots, size, size), f32),
            pltpu.VMEM((positions, rows, size), bf16),
            pltpu.VMEM((1, 128), f32),
        ),
        in_specs=[hbm] * 7,
        out_specs=(vmem, vmem, vmem, vmem),
        scratch_shapes=[
            pltpu.VMEM((per_row, row_blocks), i32),
            pltpu.VMEM((per_row, row_blocks), i32),
            pltpu.VMEM((row_blocks * per_row, rows, size), f32),
            pltpu.VMEM((slots, size, size), bf16),
            pltpu.VMEM((slots, size, size), bf16),
            pltpu.VMEM((slots, chips, rows, size), bf16),
            pltpu.VMEM((slots, chips, rows, size), bf16),
            pltpu.VMEM((slots, chips, rows, size), bf16),
            pltpu.VMEM((slots, size, size), bf16),
            pltpu.VMEM((slots, chips, 2, rows, size), bf16),
            pltpu.VMEM((slots, chips, rows, size), bf16),
            pltpu.VMEM((1, positions), i32),
            pltpu.SMEM((1, positions), i32),
            pltpu.VMEM((tensors, 1, 128), f32),
            pltpu.VMEM((chips, 1, 128), f32),
            pltpu.VMEM((2, 1, 128), f32),
            pltpu.VMEM((1, 1, 128), f32),
            dma((6 + per_row,)), *[dma] * 9, *[dma((slots,))] * 8,
        ],
        compiler_params=pltpu.CompilerParams(
            collective_id=0, has_side_effects=True, vmem_limit_bytes=32 * 2**20
        ),
        cost_estimate=pl.CostEstimate(
            flops=8 * slots * size**3, bytes_accessed=24 * 2**20, transcendentals=0
        ),
        name="exchange",
    )(*big)
    return pl.pallas_call(
        functools.partial(finish_kernel, slots),
        out_shape=(
            jax.ShapeDtypeStruct(left_gram.shape, f32),
            jax.ShapeDtypeStruct(right_gram.shape, f32),
            jax.ShapeDtypeStruct(gradient.shape, bf16),
        ),
        in_specs=[hbm, hbm, vmem, vmem, vmem, vmem],
        out_specs=(hbm, hbm, hbm),
        scratch_shapes=[
            pltpu.SMEM(owner.shape, i32),
            pltpu.SMEM(owner.shape, i32),
            pltpu.VMEM(gradient.shape, bf16),
            dma((2 * slots + 4,)),
            dma((2,)),
        ],
        compiler_params=pltpu.CompilerParams(vmem_limit_bytes=24 * 2**20),
        cost_estimate=pl.CostEstimate(flops=0, bytes_accessed=9 * 2**20, transcendentals=0),
        name="finish",
    )(*big[:2], left, right, returned, scale)


def solution(mesh):
    return jax.shard_map(
        per_device,
        mesh=mesh,
        in_specs=(
            P(None, "fsdp", "tensor"),
            P(None, "tensor"),
            P(None, "tensor"),
            P(("fsdp", "tensor"), None, None),
            P(("fsdp", "tensor"), None, None),
            P(("fsdp", "tensor"), None, None),
            P(("fsdp", "tensor"), None, None),
        ),
        out_specs=(
            P(("fsdp", "tensor"), None, None),
            P(("fsdp", "tensor"), None, None),
            P(None, "fsdp", "tensor"),
        ),
        check_vma=False,
    )
```
